256 devices in a mesh: gx: 8 (over x, core), gy: 8 (over z), gz: 4 (over y).
Axes of the slice: x: 4, y: 4, z: 8, core: 2. Of those that a mesh axis runs over, the one named last changes fastest.
Arguments:
- vec_prev: float32 [2, 1024, 128, 512], P(None, 'gx', 'gy', 'gz'), may hold values from -4 to 4
- source: float32 [2, 1024, 128, 512], P(None, 'gx', 'gy', 'gz'), may hold values from -6 to 6
- mag_mat: int32 [1024, 128, 512], P('gx', 'gy', 'gz'), may hold values from 0 to 3
- send_idx: int32 [256, 64, 128], P(('gx', 'gy', 'gz')), may hold values from 0 to 262143
- send_count: int32 [256, 64], P(('gx', 'gy', 'gz')), may hold values from 1 to 128, as said below
- recv_cell: int32 [256, 64, 128], P(('gx', 'gy', 'gz')), may hold values from 0 to 131071
- temp: float32 [256, 128, 1024], P('gx', 'gy', 'gz'), may hold values from 0 to 2
- heat_mat: int32 [256, 128, 1024], P('gx', 'gy', 'gz'), may hold values from 0 to 3
Outputs:
- potential: float32 [2, 1024, 128, 512], P(None, 'gx', 'gy', 'gz')
- temp_out: float32 [256, 128, 1024], P('gx', 'gy', 'gz')
The draws below stay inside these ranges and needn't reach their ends.
Inputs may be any that keep to these rules, and one draw needn't show every extreme that they name: `send_count`: in every draw one peer position receives 128 from every device.
All inputs are finite; a program needn't handle non-finite values.
Results may differ from the reference program's by a relative error of at most 0.00002.
Values sent between devices are 32-bit elements; how exact they have to be, the bound alone decides.
A program may use at most 128 MiB of HBM per device.

```python
import jax
import jax.numpy as jnp

MX = 128
MY = 16
MZ = 128
TX = 32
TY = 16
TZ = 256
CAP = 128
NPEER = 64
DEVICES_ALL = 256
NXM = 1024
NYM = 128
NZM = 512
NXT = 256
NYT = 128
NZT = 1024
N_GX = 8
N_GY = 8
N_GZ = 4


def draw_send_count(key, part):
    key = jax.random.fold_in(key, 1)
    first, second, third = jax.random.split(key, 3)
    rows = N_GX * N_GY * N_GZ
    upper = jax.random.randint(first, (rows, NPEER), 1, CAP + 1)
    lower = jax.random.randint(second, (rows, NPEER), 1, CAP + 1)
    counts = jnp.minimum(jnp.minimum(upper, lower) + CAP // 4, CAP)
    hottest = jax.random.randint(third, (), 0, NPEER)
    columns = jnp.arange(NPEER, dtype=jnp.int32)[None, :]
    return jnp.where(columns == hottest, CAP, counts).astype(jnp.int32)


def with_ends(array, stream_key, least, top_value):
    shape = array.shape
    place = [jax.random.randint(jax.random.fold_in(stream_key, axis), (), 0, shape[axis]) for axis in range(len(shape))]
    array = array.at[tuple(place)].set(least)
    longest = shape.index(max(shape))
    place[longest] = (place[longest] + 1) % shape[longest]
    return array.at[tuple(place)].set(top_value)


def block_levels(own_key, extent, cuts, low, top_value):
    def one(axis_at, shards_of):
        heights = jax.random.uniform(jax.random.fold_in(jax.random.fold_in(own_key, 6), axis_at), (shards_of,), jnp.float32, low / len(cuts), top_value / len(cuts))
        return jnp.repeat(jnp.exp(heights), extent[axis_at] // shards_of).reshape((-1,) + (1,) * (len(extent) - axis_at - 1))

    gain = one(*cuts[0])
    for cut in cuts[1:]:
        gain = gain * one(*cut)
    return gain


def bell_draw(rng, shape, scale, bound, shards=(), kind=jnp.bfloat16):
    array = scale * jax.random.normal(rng, shape, jnp.float32)
    if shards:
        array = array * block_levels(rng, shape, shards, -0.22, 0.18)
    return jnp.clip(array, -bound, bound).astype(kind)


def setup_inputs(seed: int = 0) -> dict:
    splits = jax.random.split(jax.random.key(seed), 9)
    vec_prev = bell_draw(splits[0], (2, NXM, NYM, NZM), 0.5, 4.0, ((1, 8), (2, 8), (3, 4)), jnp.float32)
    source = bell_draw(splits[1], (2, NXM, NYM, NZM), 1.0, 6.0, ((1, 8), (2, 8), (3, 4)), jnp.float32)
    mag_mat = with_ends(jax.random.randint(splits[2], (NXM, NYM, NZM), 0, 4), jax.random.fold_in(splits[2], 1), 0, 3).astype(jnp.int32)
    send_idx = with_ends(jax.random.randint(splits[3], (DEVICES_ALL, NPEER, CAP), 0, MX * MY * MZ), jax.random.fold_in(splits[3], 1), 0, (MX * MY * MZ) - 1).astype(jnp.int32)
    send_count = draw_send_count(jax.random.fold_in(splits[8], 71), 0)
    recv_cell = with_ends(jax.random.randint(splits[5], (DEVICES_ALL, NPEER, CAP), 0, TX * TY * TZ), jax.random.fold_in(splits[5], 1), 0, (TX * TY * TZ) - 1).astype(jnp.int32)
    temp = jnp.clip(2.0 * jax.random.uniform(splits[6], (NXT, NYT, NZT), jnp.float32) ** block_levels(splits[6], (NXT, NYT, NZT), ((0, 8), (1, 8), (2, 4)), -0.2, 0.2), 0.0, 2.0)
    heat_mat = with_ends(jax.random.randint(splits[7], (NXT, NYT, NZT), 0, 4), jax.random.fold_in(splits[7], 1), 0, 3).astype(jnp.int32)
    return {"vec_prev": vec_prev, "source": source, "mag_mat": mag_mat, "send_idx": send_idx, "send_count": send_count, "recv_cell": recv_cell, "temp": temp, "heat_mat": heat_mat}


sigma_table = (0.0, 3.0, 1.5, 6.0)
conduct_table = (1.0, 0.15, 0.05, 0.9)
capacity_table = (7.0, 2.0, 1.0, 6.0)
upwind_rate = 0.3


def lookup(material, table):
    total = jnp.zeros(material.shape, jnp.float32)
    for number in range(4):
        total = total + jnp.where(material == number, jnp.float32(table[number]), jnp.float32(0.0))
    return total


def relax(padded, sigma, source):
    beside = padded[:, 2:, 1:-1, 1:-1] + padded[:, :-2, 1:-1, 1:-1]
    beside = beside + padded[:, 1:-1, 2:, 1:-1] + padded[:, 1:-1, :-2, 1:-1]
    beside = beside + padded[:, 1:-1, 1:-1, 2:] + padded[:, 1:-1, 1:-1, :-2]
    real_part = source[0] + beside[0]
    imag_part = source[1] + beside[1]
    denom = 36.0 + sigma * sigma
    return jnp.stack([(6.0 * real_part + sigma * imag_part) / denom, (6.0 * imag_part - sigma * real_part) / denom])


def heat_step(tpad, kpad, kcell, capacity, upwind, heat_src):
    center = tpad[1:-1, 1:-1, 1:-1]
    flux = jnp.zeros(center.shape, jnp.float32)
    shifts = [(slice(2, None), slice(1, -1), slice(1, -1)), (slice(None, -2), slice(1, -1), slice(1, -1)),
              (slice(1, -1), slice(2, None), slice(1, -1)), (slice(1, -1), slice(None, -2), slice(1, -1)),
              (slice(1, -1), slice(1, -1), slice(2, None)), (slice(1, -1), slice(1, -1), slice(None, -2))]
    for where_at in shifts:
        kside = kpad[where_at]
        face = 2.0 * kcell * kside / (kcell + kside)
        flux = flux + face * (tpad[where_at] - center)
    below = tpad[1:-1, 1:-1, :-2]
    return center + (flux + heat_src) / capacity + upwind * (below - center)


def reference(vec_prev, source, mag_mat, send_idx, send_count, recv_cell, temp, heat_mat):
    sigma = lookup(mag_mat, sigma_table)
    field = vec_prev
    for sweep in range(2):
        padded = jnp.pad(field, ((0, 0), (1, 1), (1, 1), (1, 1)))
        field = relax(padded, sigma, source)
    potential = field
    loss = 0.5 * sigma * (field[0] * field[0] + field[1] * field[1])
    mcells = MX * MY * MZ
    tcells = TX * TY * TZ
    devices = N_GX * N_GY * N_GZ
    groups = N_GX * N_GY
    loss_dev = loss.reshape(N_GX, MX, N_GY, MY, N_GZ, MZ).transpose(0, 2, 4, 1, 3, 5).reshape(devices * mcells)
    offsets = (jnp.arange(devices, dtype=jnp.int32) * mcells)[:, None, None]
    values = loss_dev[(offsets + send_idx).reshape(-1)].reshape(devices, groups, CAP)
    slot_mask = jnp.arange(CAP, dtype=jnp.int32)[None, None, :] < send_count[:, :, None]
    values = jnp.where(slot_mask, values, jnp.float32(0.0))
    received = values.reshape(groups, N_GZ, groups, CAP).transpose(2, 1, 0, 3).reshape(devices, groups, CAP)
    toffsets = (jnp.arange(devices, dtype=jnp.int32) * tcells)[:, None, None]
    heat_flat = jnp.zeros((devices * tcells,), jnp.float32).at[(toffsets + recv_cell).reshape(-1)].add(received.reshape(-1))
    heat_src = heat_flat.reshape(N_GX, N_GY, N_GZ, TX, TY, TZ).transpose(0, 3, 1, 4, 2, 5).reshape(TX * N_GX, TY * N_GY, TZ * N_GZ)
    kcell = lookup(heat_mat, conduct_table)
    capacity = lookup(heat_mat, capacity_table)
    upwind = jnp.where(heat_mat == 1, jnp.float32(upwind_rate), jnp.float32(0.0))
    kpad = jnp.pad(kcell, 1)
    state = temp
    for step in range(3):
        state = heat_step(jnp.pad(state, 1), kpad, kcell, capacity, upwind, heat_src)
    return potential, state
```

```python
import jax
import jax.numpy as jnp
from jax import lax
from jax.experimental import pallas as pl
from jax.experimental.pallas import tpu as pltpu
from jax.sharding import PartitionSpec as P

sigma_table = (0.0, 3.0, 1.5, 6.0)
conduct_table = (1.0, 0.15, 0.05, 0.9)
capacity_table = (7.0, 2.0, 1.0, 6.0)
upwind_rate = 0.3
real_table = tuple(6.0 / (36.0 + s * s) for s in sigma_table)
imag_table = tuple(s / (36.0 + s * s) for s in sigma_table)
inverse_capacity = tuple(1.0 / c for c in capacity_table)

MESH = pl.DeviceIdType.MESH
LANES = 128
AXES = ("gx", "gy", "gz")
f32 = jnp.float32
bf16 = jnp.bfloat16


def lookup(material, table):
    first = jnp.where(material == 0, f32(table[0]), f32(table[1]))
    second = jnp.where(material == 2, f32(table[2]), f32(table[3]))
    return jnp.where(material < 2, first, second)


def halves(value):
    high = value.astype(bf16)
    return high, (value - high.astype(f32)).astype(bf16)


class Exchange:
    def __init__(self, number, sends, receives, faces):
        self.number, self.sends, self.receives, self.faces = number, sends, receives, faces

    def each(self):
        for at, (axis, (low_face, high_face), (low_halo, high_halo)) in enumerate(self.faces):
            me, count = lax.axis_index(axis), lax.axis_size(axis)
            up = pltpu.make_async_remote_copy(
                src_ref=high_face, dst_ref=low_halo,
                send_sem=self.sends.at[self.number, 2 * at],
                recv_sem=self.receives.at[self.number, 2 * at],
                device_id={axis: lax.rem(me + 1, count)}, device_id_type=MESH,
            )
            down = pltpu.make_async_remote_copy(
                src_ref=low_face, dst_ref=high_halo,
                send_sem=self.sends.at[self.number, 2 * at + 1],
                recv_sem=self.receives.at[self.number, 2 * at + 1],
                device_id={axis: lax.rem(me + count - 1, count)}, device_id_type=MESH,
            )
            yield me > 0, me < count - 1, up, down, low_halo, high_halo

    def start(self, only=AXES):
        for (axis, _, _), (below, above, up, down, _, _) in zip(self.faces, self.each()):
            if axis in only:
                pl.when(above)(up.start)
                pl.when(below)(down.start)

    def wait(self):
        for below, above, up, down, low_halo, high_halo in self.each():
            pl.when(below)(up.wait_recv)
            pl.when(above)(down.wait_recv)

    def clear(self):
        for axis, _, (low_halo, high_halo) in self.faces:
            me, count = lax.axis_index(axis), lax.axis_size(axis)

            @pl.when(me == 0)
            def _():
                low_halo[...] = jnp.zeros(low_halo.shape, f32)

            @pl.when(me == count - 1)
            def _():
                high_halo[...] = jnp.zeros(high_halo.shape, f32)

    def drain(self):
        for below, above, up, down, _, _ in self.each():
            pl.when(above)(up.wait_send)
            pl.when(below)(down.wait_send)


def iota(shape, dim):
    return lax.broadcasted_iota(jnp.int32, shape, dim)


def to_column(face, x):
    low = pltpu.roll(face[:, :LANES], x, 1)
    high = pltpu.roll(face[:, face.shape[1] - LANES:], lax.rem(x + 1, LANES), 1)
    return low, high


def column_shifts(plane, low, high, x):
    rows, depth = plane.shape
    lane = iota((rows, depth), 1)
    before = pltpu.roll(low, lax.rem(LANES - x, LANES), 1)
    after = pltpu.roll(high, LANES - 1 - x, 1)
    if depth > LANES:
        before = jnp.concatenate([before] * (depth // LANES), axis=1)
        after = jnp.concatenate([after] * (depth // LANES), axis=1)
    return (
        jnp.where(lane == 0, before, pltpu.roll(plane, 1, 1)),
        jnp.where(lane == depth - 1, after, pltpu.roll(plane, depth - 1, 1)),
    )


def row_shifts(plane, low, high):
    rows, depth = plane.shape
    row = iota((rows, depth), 0)
    return (
        jnp.where(row == 0, low, pltpu.roll(plane, 1, 0)),
        jnp.where(row == rows - 1, high, pltpu.roll(plane, rows - 1, 0)),
    )


def kernel(
    vec_hbm, source_hbm, mag_hbm, idx_hbm, count_ref, cell_hbm, temp_hbm, heat_hbm,
    potential_hbm, out_hbm,
    field0, field1, source, mag, idx, cell, temp0, temp1, temp2, heat_mat, kcell, coef, rate,
    ys_m, yh_m, zs_m, zh_m, ys_t, yh_t, zs_t, zh_t,
    table, chosen, sent, landed, one_hot, v_high, v_low, heat,
    load_sems, halo_send, halo_recv, slot_send, slot_recv,
):
    _, size_x, size_y, size_z = source.shape
    heat_x, heat_y, heat_z = heat_mat.shape
    n_gx, n_gy = lax.axis_size("gx"), lax.axis_size("gy")
    ix, iy, iz, n_gz = lax.axis_index("gx"), lax.axis_index("gy"), lax.axis_index("gz"), lax.axis_size("gz")
    group, here = n_gx * n_gy, ix * n_gy + iy

    loads = [
        pltpu.make_async_copy(src, dst, load_sems.at[at])
        for at, (src, dst) in enumerate(
            [
                (vec_hbm, field0.at[:, pl.ds(1, size_x)]),
                (temp_hbm, temp0.at[pl.ds(1, heat_x)]),
                (heat_hbm, heat_mat),
                (mag_hbm, mag),
                (source_hbm, source),
                (idx_hbm.at[0], idx),
                (cell_hbm.at[0], cell),
            ]
        )
    ]
    for load in loads:
        load.start()

    barrier = pltpu.get_barrier_semaphore()

    @pl.loop(1, group)
    def _(step):
        peer = lax.rem(here + step, group)
        pl.semaphore_signal(
            barrier, inc=1, device_id={"gx": peer // n_gy, "gy": lax.rem(peer, n_gy)}, device_id_type=MESH
        )

    @pl.when(iz > 0)
    def _():
        pl.semaphore_signal(barrier, inc=1, device_id={"gz": lax.rem(iz + n_gz - 1, n_gz)}, device_id_type=MESH)

    @pl.when(iz < n_gz - 1)
    def _():
        pl.semaphore_signal(barrier, inc=1, device_id={"gz": lax.rem(iz + 1, n_gz)}, device_id_type=MESH)

    def faces(x_low, x_high, x_low_halo, x_high_halo, ys, yh, zs, zh, at):
        return [
            ("gx", (x_low, x_high), (x_low_halo, x_high_halo)),
            ("gy", (ys.at[at, 0], ys.at[at, 1]), (yh.at[at, 0], yh.at[at, 1])),
            ("gz", (zs.at[at, 0], zs.at[at, 1]), (zh.at[at, 0], zh.at[at, 1])),
        ]

    def mag_round(number, field, x_from):
        return Exchange(
            number, halo_send, halo_recv,
            faces(*x_from, field.at[:, 0], field.at[:, size_x + 1], ys_m, yh_m, zs_m, zh_m, number),
        )

    def heat_round(number, at, state):
        return Exchange(
            number, halo_send, halo_recv,
            faces(
                state.at[1], state.at[heat_x], state.at[0], state.at[heat_x + 1],
                ys_t, yh_t, zs_t, zh_t, at,
            ),
        )

    round0 = mag_round(0, field0, (vec_hbm.at[:, 0], vec_hbm.at[:, size_x - 1]))
    round1 = mag_round(1, field1, (field1.at[:, 1], field1.at[:, size_x]))
    round_t = heat_round(2, 0, temp0)
    round_k = heat_round(3, 1, kcell)
    round_1 = heat_round(4, 2, temp1)
    round_2 = heat_round(5, 3, temp2)
    rounds = (round0, round1, round_t, round_k, round_1, round_2)
    for each in rounds:
        each.clear()

    zero_m = jnp.zeros((size_y, LANES), f32)
    zero_t = jnp.zeros((heat_y, LANES), f32)
    lane_m = iota((size_y, LANES), 1)
    lane_t = iota((heat_y, LANES), 1)

    def pack_mag(at, x, planes, columns):
        result = []
        for part in range(2):
            ys_m[at, 0, part, x] = planes[part][0:1, :]
            ys_m[at, 1, part, x] = planes[part][size_y - 1:size_y, :]
            low, high = to_column(planes[part], x)
            result.append(jnp.where(lane_m == x, low, columns[2 * part]))
            result.append(jnp.where(lane_m == x, high, columns[2 * part + 1]))
        return tuple(result)

    def store_mag(at, columns):
        for part in range(2):
            zs_m[at, 0, part] = columns[2 * part]
            zs_m[at, 1, part] = columns[2 * part + 1]

    def pack_heat(at, x, plane, columns):
        ys_t[at, 0, x] = plane[0:1, :]
        ys_t[at, 1, x] = plane[heat_y - 1:heat_y, :]
        low, high = to_column(plane, x)
        return (
            jnp.where(lane_t == x, low, columns[0]),
            jnp.where(lane_t == x, high, columns[1]),
        )

    def store_heat(at, columns):
        zs_t[at, 0] = columns[0]
        zs_t[at, 1] = columns[1]

    loads[0].wait()
    columns = lax.fori_loop(
        0, size_x,
        lambda x, carry: pack_mag(0, x, (field0[0, x + 1], field0[1, x + 1]), carry),
        (zero_m,) * 4, unroll=4,
    )
    store_mag(0, columns)
    pl.semaphore_wait(barrier, group - 1 + (iz > 0).astype(jnp.int32) + (iz < n_gz - 1).astype(jnp.int32))
    round0.start()

    loads[1].wait()
    loads[2].wait()

    def pack_thermal(x, carry):
        conduct = lookup(heat_mat[x], conduct_table)
        kcell[x + 1] = conduct
        return pack_heat(0, x, temp0[x + 1], carry[:2]) + pack_heat(1, x, conduct, carry[2:])

    columns = lax.fori_loop(0, heat_x, pack_thermal, (zero_t,) * 4, unroll=4)
    store_heat(0, columns[:2])
    store_heat(1, columns[2:])
    round_t.start()
    round_k.start()
    for load in loads[3:]:
        load.wait()

    def relaxed(at, field, x, columns):
        total = []
        for part in range(2):
            plane = field[part, x + 1]
            low_y, high_y = row_shifts(plane, yh_m[at, 0, part, x], yh_m[at, 1, part, x])
            low_z, high_z = column_shifts(plane, columns[2 * part], columns[2 * part + 1], x)
            total.append(
                source[part, x] + ((field[part, x] + field[part, x + 2]) + (low_y + high_y) + (low_z + high_z))
            )
        material = mag[x]
        real, imag = lookup(material, real_table), lookup(material, imag_table)
        return real * total[0] + imag * total[1], real * total[1] - imag * total[0]

    def halo_columns(at):
        return (zh_m[at, 0, 0], zh_m[at, 1, 0], zh_m[at, 0, 1], zh_m[at, 1, 1])

    round0.wait()
    halo0 = halo_columns(0)

    def first_sweep(x, carry):
        planes = relaxed(0, field0, x, halo0)
        field1[0, x + 1] = planes[0]
        field1[1, x + 1] = planes[1]
        return pack_mag(1, x, planes, carry)

    store_mag(1, lax.fori_loop(0, size_x, first_sweep, (zero_m,) * 4, unroll=2))
    round1.start()

    round_t.wait()
    round_k.wait()

    def neighbours(at, state, x, columns):
        plane = state[x + 1]
        low_y, high_y = row_shifts(plane, yh_t[at, 0, x], yh_t[at, 1, x])
        low_z, high_z = column_shifts(plane, columns[0], columns[1], x)
        return plane, (state[x], state[x + 2], low_y, high_y, low_z, high_z)

    halo_k = (zh_t[1, 0], zh_t[1, 1])
    halo_t = (zh_t[0, 0], zh_t[0, 1])

    @pl.loop(0, heat_x)
    def _(x):
        material = heat_mat[x]
        conduct, beside = neighbours(1, kcell, x, halo_k)
        inverse = lookup(material, inverse_capacity)
        upwind = jnp.where(material == 1, f32(upwind_rate), f32(0.0))
        twice = (2.0 * inverse) * conduct
        centre = 1.0 - upwind
        weights = []
        for side, other in enumerate(beside):
            weight = twice * other / (conduct + other)
            centre = centre - weight
            if side == 4:
                weight = weight + upwind
            coef[side, x] = weight
            weights.append(weight)
        coef[6, x] = centre
        rate[x] = inverse
        plane, around = neighbours(0, temp0, x, halo_t)
        total = centre * plane
        for weight, other in zip(weights, around):
            total = total + weight * other
        temp1[x + 1] = total

    round1.wait()
    halo1 = halo_columns(1)
    block = LANES // size_y

    @pl.loop(0, size_x // block)
    def _(j):
        losses = []
        for i in range(block):
            x = j * block + i
            planes = relaxed(1, field1, x, halo1)
            field0[0, x + 1] = planes[0]
            field0[1, x + 1] = planes[1]
            losses.append(
                (0.5 * lookup(mag[x], sigma_table)) * (planes[0] * planes[0] + planes[1] * planes[1])
            )
        high, low = halves(jnp.transpose(jnp.concatenate(losses, axis=0)))
        at = pl.ds(pl.multiple_of(j * LANES, LANES), LANES)
        table[0:size_z, at] = high
        table[size_z:2 * size_z, at] = low

    store_potential = pltpu.make_async_copy(
        field0.at[:, pl.ds(1, size_x)], potential_hbm, load_sems.at[7]
    )
    store_potential.start()

    table_rows = size_x * size_y
    width = n_gy * LANES
    slot = iota((1, LANES), 1)
    row16 = lax.broadcasted_iota(jnp.int16, (table_rows, LANES), 0)
    sub_z = iota((size_z, LANES), 0)

    def slot_copy(peer, source_slot):
        return pltpu.make_async_remote_copy(
            src_ref=sent.at[peer], dst_ref=landed.at[source_slot],
            send_sem=slot_send.at[peer], recv_sem=slot_recv.at[source_slot],
            device_id={"gx": peer // n_gy, "gy": lax.rem(peer, n_gy)}, device_id_type=MESH,
        )

    @pl.loop(0, n_gx)
    def _(step):
        first = lax.rem(ix + step + 1, n_gx) * n_gy
        cells = []
        for p in range(n_gy):
            wanted = jnp.where(slot < count_ref[0, first + p], idx[pl.ds(first + p, 1), :], -1)
            cells.append(wanted)
            row = jnp.broadcast_to(lax.shift_right_arithmetic(wanted, 7).astype(jnp.int16), (table_rows, LANES))
            chosen[:, LANES * p:LANES * (p + 1)] = jnp.where(row16 == row, jnp.ones((), bf16), jnp.zeros((), bf16))
        found = jnp.dot(table[...], chosen[...], preferred_element_type=f32)
        found = found[:size_z] + found[size_z:]
        for p in range(n_gy):
            hit = sub_z == (cells[p] & (size_z - 1))
            sent[first + p] = jnp.sum(
                jnp.where(hit, found[:, LANES * p:LANES * (p + 1)], 0.0), axis=0, keepdims=True
            )
        for p in range(n_gy):
            @pl.when(first + p != here)
            def _():
                slot_copy(first + p, here).start()

    landed[here] = sent[here]

    row_h = lax.broadcasted_iota(jnp.int16, (heat_x * heat_y, LANES), 0)
    row_z = lax.broadcasted_iota(jnp.int16, (heat_z, LANES), 0)
    shift = heat_z.bit_length() - 1
    heat[...] = jnp.zeros(heat.shape, f32)
    per = one_hot.shape[1] // LANES
    zero16 = jnp.zeros((), bf16)
    transposed = (((1,), (1,)), ((), ()))

    @pl.loop(0, group // per)
    def _(step):
        for p in range(per):
            peer = step * per + p

            @pl.when(peer != here)
            def _():
                slot_copy(peer, peer).wait_recv()

        for p in range(per):
            peer = step * per + p
            target = cell[pl.ds(peer, 1), :]
            high, low = halves(landed[peer])
            at = slice(LANES * p, LANES * (p + 1))
            row = jnp.broadcast_to(lax.shift_right_logical(target, shift).astype(jnp.int16), row_h.shape)
            one_hot[:, at] = jnp.where(row_h == row, jnp.ones((), bf16), zero16)
            hit = row_z == jnp.broadcast_to((target & (heat_z - 1)).astype(jnp.int16), row_z.shape)
            v_high[:, at] = jnp.where(hit, jnp.broadcast_to(high, row_z.shape), zero16)
            v_low[:, at] = jnp.where(hit, jnp.broadcast_to(low, row_z.shape), zero16)
        heat[...] += lax.dot_general(
            one_hot[...], v_high[...], transposed, preferred_element_type=f32
        ) + lax.dot_general(one_hot[...], v_low[...], transposed, preferred_element_type=f32)

    def first_step(x, carry):
        gain = heat[pl.ds(pl.multiple_of(x * heat_y, heat_y), heat_y), :] * rate[x]
        rate[x] = gain
        plane = temp1[x + 1] + gain
        temp1[x + 1] = plane
        return pack_heat(2, x, plane, carry)

    store_heat(2, lax.fori_loop(0, heat_x, first_step, (zero_t,) * 2, unroll=2))
    round_1.start()
    round_t.drain()

    def stepped(at, state, x, columns):
        plane, around = neighbours(at, state, x, columns)
        total = coef[6, x] * plane + rate[x]
        for side, other in enumerate(around):
            total = total + coef[side, x] * other
        return total

    round_1.wait()
    halo_1 = (zh_t[2, 0], zh_t[2, 1])

    def second_step(x, carry):
        plane = stepped(2, temp1, x, halo_1)
        temp2[x + 1] = plane
        return pack_heat(3, x, plane, carry)

    store_heat(3, lax.fori_loop(0, heat_x, second_step, (zero_t,) * 2, unroll=2))
    round_2.start()
    round_2.wait()
    halo_2 = (zh_t[3, 0], zh_t[3, 1])

    @pl.loop(0, heat_x)
    def _(x):
        temp0[x + 1] = stepped(3, temp2, x, halo_2)

    store_temp = pltpu.make_async_copy(temp0.at[pl.ds(1, heat_x)], out_hbm, load_sems.at[8])
    store_temp.start()
    for each in (round0, round1, round_k, round_1, round_2):
        each.drain()

    @pl.loop(0, group)
    def _(peer):
        @pl.when(peer != here)
        def _():
            slot_copy(peer, here).wait_send()

    store_potential.wait()
    store_temp.wait()


def shards(vec_prev, source, mag_mat, send_idx, send_count, recv_cell, temp, heat_mat):
    _, size_x, size_y, size_z = vec_prev.shape
    heat_x, heat_y, heat_z = temp.shape
    n_gy = lax.axis_size("gy")
    group = lax.axis_size("gx") * n_gy
    per = min(16, group)
    vmem = pltpu.VMEM
    anywhere = pl.BlockSpec(memory_space=pl.ANY)
    return pl.pallas_call(
        kernel,
        out_shape=(
            jax.ShapeDtypeStruct(vec_prev.shape, f32),
            jax.ShapeDtypeStruct(temp.shape, f32),
        ),
        in_specs=[anywhere] * 4 + [pl.BlockSpec(memory_space=pltpu.SMEM)] + [anywhere] * 3,
        out_specs=(anywhere, anywhere),
        scratch_shapes=[
            vmem((2, size_x + 2, size_y, size_z), f32),
            vmem((2, size_x + 2, size_y, size_z), f32),
            vmem(source.shape, f32),
            vmem(mag_mat.shape, jnp.int32),
            vmem(send_idx.shape[1:], jnp.int32),
            vmem(recv_cell.shape[1:], jnp.int32),
            vmem((heat_x + 2, heat_y, heat_z), f32),
            vmem((heat_x + 2, heat_y, heat_z), f32),
            vmem((heat_x + 2, heat_y, heat_z), f32),
            vmem(heat_mat.shape, jnp.int32),
            vmem((heat_x + 2, heat_y, heat_z), f32),
            vmem((7, heat_x, heat_y, heat_z), f32),
            vmem((heat_x, heat_y, heat_z), f32),
            vmem((2, 2, 2, size_x, 1, size_z), f32),
            vmem((2, 2, 2, size_x, 1, size_z), f32),
            vmem((2, 2, 2, size_y, LANES), f32),
            vmem((2, 2, 2, size_y, LANES), f32),
            vmem((4, 2, heat_x, 1, heat_z), f32),
            vmem((4, 2, heat_x, 1, heat_z), f32),
            vmem((4, 2, heat_y, LANES), f32),
            vmem((4, 2, heat_y, LANES), f32),
            vmem((2 * size_z, size_x * size_y), bf16),
            vmem((size_x * size_y, n_gy * LANES), bf16),
            vmem((group, 1, LANES), f32),
            vmem((group, 1, LANES), f32),
            vmem((heat_x * heat_y, per * LANES), bf16),
            vmem((heat_z, per * LANES), bf16),
            vmem((heat_z, per * LANES), bf16),
            vmem((heat_x * heat_y, heat_z), f32),
            pltpu.SemaphoreType.DMA((9,)),
            pltpu.SemaphoreType.DMA((6, 6)),
            pltpu.SemaphoreType.DMA((6, 6)),
            pltpu.SemaphoreType.DMA((group,)),
            pltpu.SemaphoreType.DMA((group,)),
        ],
        compiler_params=pltpu.CompilerParams(
            collective_id=0, has_side_effects=True, vmem_limit_bytes=56 << 20
        ),
    )(vec_prev, source, mag_mat, send_idx, send_count, recv_cell, temp, heat_mat)


def solution(mesh):
    placed = (
        P(None, "gx", "gy", "gz"),
        P(None, "gx", "gy", "gz"),
        P("gx", "gy", "gz"),
        P(("gx", "gy", "gz"), None, None),
        P(("gx", "gy", "gz"), None),
        P(("gx", "gy", "gz"), None, None),
        P("gx", "gy", "gz"),
        P("gx", "gy", "gz"),
    )
    return jax.shard_map(
        shards,
        mesh=mesh,
        in_specs=placed,
        out_specs=(P(None, "gx", "gy", "gz"), P("gx", "gy", "gz")),
        check_vma=False,
    )
```

```python
import jax
import jax.numpy as jnp
from jax import lax
from jax.experimental import pallas as pl
from jax.experimental.pallas import tpu as pltpu
from jax.sharding import PartitionSpec as P

sigma_table = (0.0, 3.0, 1.5, 6.0)
conduct_table = (1.0, 0.15, 0.05, 0.9)
capacity_table = (7.0, 2.0, 1.0, 6.0)
upwind_rate = 0.3
real_table = tuple(6.0 / (36.0 + s * s) for s in sigma_table)
imag_table = tuple(s / (36.0 + s * s) for s in sigma_table)
inverse_capacity = tuple(1.0 / c for c in capacity_table)

MESH = pl.DeviceIdType.MESH
LANES = 128
AXES = ("gx", "gy", "gz")
f32 = jnp.float32
bf16 = jnp.bfloat16


def lookup(material, table):
    first = jnp.where(material == 0, f32(table[0]), f32(table[1]))
    second = jnp.where(material == 2, f32(table[2]), f32(table[3]))
    return jnp.where(material < 2, first, second)


def halves(value):
    high = value.astype(bf16)
    return high, (value - high.astype(f32)).astype(bf16)


class Exchange:
    def __init__(self, number, sends, receives, faces):
        self.number, self.sends, self.receives, self.faces = number, sends, receives, faces

    def each(self):
        for at, (axis, (low_face, high_face), (low_halo, high_halo)) in enumerate(self.faces):
            me, count = lax.axis_index(axis), lax.axis_size(axis)
            up = pltpu.make_async_remote_copy(
                src_ref=high_face, dst_ref=low_halo,
                send_sem=self.sends.at[self.number, 2 * at],
                recv_sem=self.receives.at[self.number, 2 * at],
                device_id={axis: wrap(me + 1, count)}, device_id_type=MESH,
            )
            down = pltpu.make_async_remote_copy(
                src_ref=low_face, dst_ref=high_halo,
                send_sem=self.sends.at[self.number, 2 * at + 1],
                recv_sem=self.receives.at[self.number, 2 * at + 1],
                device_id={axis: wrap(me + count - 1, count)}, device_id_type=MESH,
            )
            yield me > 0, me < count - 1, up, down, low_halo, high_halo

    def start(self, only=AXES):
        for (axis, _, _), (below, above, up, down, _, _) in zip(self.faces, self.each()):
            if axis in only:
                pl.when(above)(up.start)
                pl.when(below)(down.start)

    def wait(self):
        for below, above, up, down, low_halo, high_halo in self.each():
            pl.when(below)(up.wait_recv)
            pl.when(above)(down.wait_recv)

    def clear(self):
        for axis, _, (low_halo, high_halo) in self.faces:
            me, count = lax.axis_index(axis), lax.axis_size(axis)

            @pl.when(me == 0)
            def _():
                low_halo[...] = jnp.zeros(low_halo.shape, f32)

            @pl.when(me == count - 1)
            def _():
                high_halo[...] = jnp.zeros(high_halo.shape, f32)

    def drain(self):
        for below, above, up, down, _, _ in self.each():
            pl.when(above)(up.wait_send)
            pl.when(below)(down.wait_send)


def iota(shape, dim):
    return lax.broadcasted_iota(jnp.int32, shape, dim)


def wrap(value, count):
    return value & (count - 1) if count & (count - 1) == 0 else lax.rem(value, count)


def face_columns(planes):
    stacked = jnp.concatenate(planes, axis=0)
    depth = stacked.shape[1]
    low = jnp.transpose(stacked[:, :LANES])
    high = low if depth == LANES else jnp.transpose(stacked[:, depth - LANES:])
    return low[0:1, :], high[LANES - 1:LANES, :]


def halo_columns(low, high):
    sub = iota((LANES, LANES), 0)
    return jnp.transpose(jnp.where(sub == 0, low, jnp.where(sub == LANES - 1, high, f32(0.0))))


def column_shifts(plane, halo):
    rows, depth = plane.shape
    lane = iota((rows, depth), 1)
    if depth > LANES:
        halo = jnp.concatenate([halo] * (depth // LANES), axis=1)
    return (
        jnp.where(lane == 0, halo, pltpu.roll(plane, 1, 1)),
        jnp.where(lane == depth - 1, halo, pltpu.roll(plane, depth - 1, 1)),
    )


def row_shifts(plane, low, high):
    rows, depth = plane.shape
    row = iota((rows, depth), 0)
    return (
        jnp.where(row == 0, low, pltpu.roll(plane, 1, 0)),
        jnp.where(row == rows - 1, high, pltpu.roll(plane, rows - 1, 0)),
    )


def kernel(
    vec_hbm, source_hbm, mag_hbm, idx_hbm, count_hbm, cell_hbm, temp_hbm, heat_hbm,
    potential_hbm, out_hbm,
    field0, field1, source, mag, idx, count_ref, cell, temp0, temp1, temp2, heat_mat, kcell, coef, rate,
    ys_m, yh_m, zs_m, zh_m, ys_t, yh_t, zs_t, zh_t,
    table, chosen, sent, landed, one_hot, v_high, v_low, heat,
    load_sems, halo_send, halo_recv, slot_send, slot_recv,
):
    _, size_x, size_y, size_z = source.shape
    heat_x, heat_y, heat_z = heat_mat.shape
    n_gx, n_gy = lax.axis_size("gx"), lax.axis_size("gy")
    ix, iy, iz, n_gz = lax.axis_index("gx"), lax.axis_index("gy"), lax.axis_index("gz"), lax.axis_size("gz")
    group, here = n_gx * n_gy, ix * n_gy + iy

    loads = [
        pltpu.make_async_copy(src, dst, load_sems.at[at])
        for at, (src, dst) in enumerate(
            [
                (vec_hbm, field0.at[:, pl.ds(1, size_x)]),
                (temp_hbm, temp0.at[pl.ds(1, heat_x)]),
                (heat_hbm, heat_mat),
                (mag_hbm, mag),
                (source_hbm, source),
                (idx_hbm.at[0], idx),
                (cell_hbm.at[0], cell),
                (count_hbm, count_ref),
            ]
        )
    ]
    for load in loads:
        load.start()

    barrier = pltpu.get_barrier_semaphore()

    def greet(device):
        pl.semaphore_signal(barrier, inc=1, device_id=device, device_id_type=MESH)

    for step in range(1, n_gy):
        greet({"gy": wrap(iy + step, n_gy)})

    @pl.loop(1, n_gx)
    def _(step):
        for other in range(n_gy):
            greet({"gx": wrap(ix + step, n_gx), "gy": other})

    @pl.when(iz > 0)
    def _():
        greet({"gz": wrap(iz + n_gz - 1, n_gz)})

    @pl.when(iz < n_gz - 1)
    def _():
        greet({"gz": wrap(iz + 1, n_gz)})

    def faces(x_low, x_high, x_low_halo, x_high_halo, ys, yh, zs, zh, at):
        return [
            ("gx", (x_low, x_high), (x_low_halo, x_high_halo)),
            ("gy", (ys.at[at, 0], ys.at[at, 1]), (yh.at[at, 0], yh.at[at, 1])),
            ("gz", (zs.at[at, 0], zs.at[at, 1]), (zh.at[at, 0], zh.at[at, 1])),
        ]

    def mag_round(number, field, x_from):
        return Exchange(
            number, halo_send, halo_recv,
            faces(*x_from, field.at[:, 0], field.at[:, size_x + 1], ys_m, yh_m, zs_m, zh_m, number),
        )

    def heat_round(number, at, state):
        return Exchange(
            number, halo_send, halo_recv,
            faces(
                state.at[1], state.at[heat_x], state.at[0], state.at[heat_x + 1],
                ys_t, yh_t, zs_t, zh_t, at,
            ),
        )

    round0 = mag_round(0, field0, (vec_hbm.at[:, 0], vec_hbm.at[:, size_x - 1]))
    round1 = mag_round(1, field1, (field1.at[:, 1], field1.at[:, size_x]))
    round_t = heat_round(2, 0, temp0)
    round_k = heat_round(3, 1, kcell)
    round_1 = heat_round(4, 2, temp1)
    round_2 = heat_round(5, 3, temp2)
    rounds = (round0, round1, round_t, round_k, round_1, round_2)
    for each in rounds:
        each.clear()

    block = LANES // size_y
    block_t = LANES // heat_y

    def pack_mag(at, j, part, planes):
        for i, plane in enumerate(planes):
            ys_m[at, 0, part, j * block + i] = plane[0:1, :]
            ys_m[at, 1, part, j * block + i] = plane[size_y - 1:size_y, :]
        zs_m[at, 0, part, j], zs_m[at, 1, part, j] = face_columns(planes)

    def pack_heat(at, j, planes):
        for i, plane in enumerate(planes):
            ys_t[at, 0, j * block_t + i] = plane[0:1, :]
            ys_t[at, 1, j * block_t + i] = plane[heat_y - 1:heat_y, :]
        zs_t[at, 0, j], zs_t[at, 1, j] = face_columns(planes)

    loads[0].wait()

    @pl.loop(0, size_x // block)
    def _(j):
        for part in range(2):
            pack_mag(0, j, part, [field0[part, j * block + i + 1] for i in range(block)])

    pl.semaphore_wait(barrier, group - 1 + (iz > 0).astype(jnp.int32) + (iz < n_gz - 1).astype(jnp.int32))
    round0.start()

    loads[1].wait()
    loads[2].wait()

    @pl.loop(0, heat_x // block_t)
    def _(j):
        planes = []
        for i in range(block_t):
            x = j * block_t + i
            planes.append(lookup(heat_mat[x], conduct_table))
            kcell[x + 1] = planes[-1]
        pack_heat(1, j, planes)
        pack_heat(0, j, [temp0[j * block_t + i + 1] for i in range(block_t)])

    round_t.start()
    round_k.start()
    for load in loads[3:]:
        load.wait()

    def relaxed(at, field, j):
        columns = [halo_columns(zh_m[at, 0, part, j], zh_m[at, 1, part, j]) for part in range(2)]
        result = ([], [])
        for i in range(block):
            x = j * block + i
            total = []
            for part in range(2):
                plane = field[part, x + 1]
                low_y, high_y = row_shifts(plane, yh_m[at, 0, part, x], yh_m[at, 1, part, x])
                low_z, high_z = column_shifts(plane, columns[part][i * size_y:(i + 1) * size_y, :])
                total.append(
                    source[part, x] + ((field[part, x] + field[part, x + 2]) + (low_y + high_y) + (low_z + high_z))
                )
            material = mag[x]
            real, imag = lookup(material, real_table), lookup(material, imag_table)
            result[0].append(real * total[0] + imag * total[1])
            result[1].append(real * total[1] - imag * total[0])
        return result

    round0.wait()

    @pl.loop(0, size_x // block)
    def _(j):
        for part, planes in enumerate(relaxed(0, field0, j)):
            for i, plane in enumerate(planes):
                field1[part, j * block + i + 1] = plane
            pack_mag(1, j, part, planes)

    round1.start()

    round_t.wait()
    round_k.wait()

    def neighbours(at, state, j):
        columns = halo_columns(zh_t[at, 0, j], zh_t[at, 1, j])
        for i in range(block_t):
            x = j * block_t + i
            plane = state[x + 1]
            low_y, high_y = row_shifts(plane, yh_t[at, 0, x], yh_t[at, 1, x])
            low_z, high_z = column_shifts(plane, columns[i * heat_y:(i + 1) * heat_y, :])
            yield x, plane, (state[x], state[x + 2], low_y, high_y, low_z, high_z)

    @pl.loop(0, heat_x // block_t)
    def _(j):
        for (x, conduct, beside), (_, plane, around) in zip(neighbours(1, kcell, j), neighbours(0, temp0, j)):
            material = heat_mat[x]
            inverse = lookup(material, inverse_capacity)
            upwind = jnp.where(material == 1, f32(upwind_rate), f32(0.0))
            twice = (2.0 * inverse) * conduct
            centre = 1.0 - upwind
            total = jnp.zeros(plane.shape, f32)
            for side in range(6):
                weight = twice * beside[side] / (conduct + beside[side])
                centre = centre - weight
                if side == 4:
                    weight = weight + upwind
                coef[side, x] = weight
                total = total + weight * around[side]
            coef[6, x] = centre
            rate[x] = inverse
            temp1[x + 1] = total + centre * plane

    round1.wait()

    @pl.loop(0, size_x // block)
    def _(j):
        losses = []
        for i, planes in enumerate(zip(*relaxed(1, field1, j))):
            x = j * block + i
            field0[0, x + 1] = planes[0]
            field0[1, x + 1] = planes[1]
            losses.append(
                (0.5 * lookup(mag[x], sigma_table)) * (planes[0] * planes[0] + planes[1] * planes[1])
            )
        high, low = halves(jnp.transpose(jnp.concatenate(losses, axis=0)))
        at = pl.ds(pl.multiple_of(j * LANES, LANES), LANES)
        table[0:size_z, at] = high
        table[size_z:2 * size_z, at] = low

    store_potential = pltpu.make_async_copy(
        field0.at[:, pl.ds(1, size_x)], potential_hbm, load_sems.at[8]
    )
    store_potential.start()

    table_rows = size_x * size_y
    width = n_gy * LANES
    slot = iota((1, LANES), 1)
    row16 = lax.broadcasted_iota(jnp.int16, (table_rows, LANES), 0)
    sub_z = iota((size_z, LANES), 0)

    def slot_copy(gx, gy):
        return pltpu.make_async_remote_copy(
            src_ref=sent.at[gx * n_gy + gy], dst_ref=landed.at[here],
            send_sem=slot_send, recv_sem=slot_recv.at[ix],
            device_id={"gx": gx, "gy": gy}, device_id_type=MESH,
        )

    def slots_from(gx, count):
        rows = landed.at[pl.ds(gx * n_gy, count)]
        return pltpu.make_async_remote_copy(
            src_ref=rows, dst_ref=rows, send_sem=slot_send, recv_sem=slot_recv.at[gx],
            device_id={"gx": wrap(ix + 1, n_gx)}, device_id_type=MESH,
        )

    @pl.loop(0, n_gx)
    def _(step):
        target = wrap(ix + step + 1, n_gx)
        first = target * n_gy
        cells = []
        for p in range(n_gy):
            wanted = jnp.where(slot < count_ref[0, first + p], idx[pl.ds(first + p, 1), :], -1)
            cells.append(wanted)
            row = jnp.broadcast_to(lax.shift_right_arithmetic(wanted, 7).astype(jnp.int16), (table_rows, LANES))
            chosen[:, LANES * p:LANES * (p + 1)] = jnp.where(row16 == row, jnp.ones((), bf16), jnp.zeros((), bf16))
        found = jnp.dot(table[...], chosen[...], preferred_element_type=f32)
        found = found[:size_z] + found[size_z:]
        for p in range(n_gy):
            hit = sub_z == (cells[p] & (size_z - 1))
            sent[first + p] = jnp.sum(
                jnp.where(hit, found[:, LANES * p:LANES * (p + 1)], 0.0), axis=0, keepdims=True
            )
        for p in range(n_gy):
            @pl.when(first + p != here)
            def _():
                slot_copy(target, p).start()

    landed[here] = sent[here]

    row_h = lax.broadcasted_iota(jnp.int16, (heat_x * heat_y, LANES), 0)
    row_z = lax.broadcasted_iota(jnp.int16, (heat_z, LANES), 0)
    shift = heat_z.bit_length() - 1
    heat[...] = jnp.zeros(heat.shape, f32)
    per = one_hot.shape[1] // LANES // n_gy
    zero16 = jnp.zeros((), bf16)
    transposed = (((1,), (1,)), ((), ()))

    @pl.loop(0, n_gx // per)
    def _(step):
        peers = []
        for k in range(per):
            gx = wrap(ix + 2 * n_gx - 1 - (step * per + k), n_gx)

            @pl.when(gx != ix)
            def _():
                slots_from(gx, n_gy).wait_recv()

            @pl.when(gx == ix)
            def _():
                slots_from(gx, n_gy - 1).wait_recv()

            peers += [gx * n_gy + gy for gy in range(n_gy)]

        for p, peer in enumerate(peers):
            target = cell[pl.ds(peer, 1), :]
            high, low = halves(landed[peer])
            at = slice(LANES * p, LANES * (p + 1))
            row = jnp.broadcast_to(lax.shift_right_logical(target, shift).astype(jnp.int16), row_h.shape)
            one_hot[:, at] = jnp.where(row_h == row, jnp.ones((), bf16), zero16)
            hit = row_z == jnp.broadcast_to((target & (heat_z - 1)).astype(jnp.int16), row_z.shape)
            v_high[:, at] = jnp.where(hit, jnp.broadcast_to(high, row_z.shape), zero16)
            v_low[:, at] = jnp.where(hit, jnp.broadcast_to(low, row_z.shape), zero16)
        heat[...] += lax.dot_general(
            one_hot[...], v_high[...], transposed, preferred_element_type=f32
        ) + lax.dot_general(one_hot[...], v_low[...], transposed, preferred_element_type=f32)

    @pl.loop(0, heat_x // block_t)
    def _(j):
        planes = []
        for i in range(block_t):
            x = j * block_t + i
            gain = heat[pl.ds(pl.multiple_of(x * heat_y, heat_y), heat_y), :] * rate[x]
            rate[x] = gain
            planes.append(temp1[x + 1] + gain)
            temp1[x + 1] = planes[-1]
        pack_heat(2, j, planes)

    round_1.start()
    round_t.drain()

    def stepped(at, state, j):
        for x, plane, around in neighbours(at, state, j):
            total = coef[6, x] * plane + rate[x]
            for side, other in enumerate(around):
                total = total + coef[side, x] * other
            yield x, total

    round_1.wait()

    @pl.loop(0, heat_x // block_t)
    def _(j):
        planes = []
        for x, plane in stepped(2, temp1, j):
            temp2[x + 1] = plane
            planes.append(plane)
        pack_heat(3, j, planes)

    round_2.start()
    round_2.wait()

    @pl.loop(0, heat_x // block_t)
    def _(j):
        for x, plane in stepped(3, temp2, j):
            temp0[x + 1] = plane

    store_temp = pltpu.make_async_copy(temp0.at[pl.ds(1, heat_x)], out_hbm, load_sems.at[9])
    store_temp.start()
    for each in (round0, round1, round_k, round_1, round_2):
        each.drain()

    everyone = sent.at[pl.ds(0, group - 1)]
    pltpu.make_async_remote_copy(
        src_ref=everyone, dst_ref=everyone, send_sem=slot_send, recv_sem=slot_recv.at[0],
        device_id={"gx": wrap(ix + 1, n_gx)}, device_id_type=MESH,
    ).wait_send()
    store_potential.wait()
    store_temp.wait()


def shards(vec_prev, source, mag_mat, send_idx, send_count, recv_cell, temp, heat_mat):
    _, size_x, size_y, size_z = vec_prev.shape
    heat_x, heat_y, heat_z = temp.shape
    n_gx, n_gy = lax.axis_size("gx"), lax.axis_size("gy")
    group = n_gx * n_gy
    per = min(2, n_gx) * n_gy
    vmem = pltpu.VMEM
    anywhere = pl.BlockSpec(memory_space=pl.ANY)
    return pl.pallas_call(
        kernel,
        out_shape=(
            jax.ShapeDtypeStruct(vec_prev.shape, f32),
            jax.ShapeDtypeStruct(temp.shape, f32),
        ),
        in_specs=[anywhere] * 8,
        out_specs=(anywhere, anywhere),
        scratch_shapes=[
            vmem((2, size_x + 2, size_y, size_z), f32),
            vmem((2, size_x + 2, size_y, size_z), f32),
            vmem(source.shape, f32),
            vmem(mag_mat.shape, jnp.int32),
            vmem(send_idx.shape[1:], jnp.int32),
            pltpu.SMEM(send_count.shape, jnp.int32),
            vmem(recv_cell.shape[1:], jnp.int32),
            vmem((heat_x + 2, heat_y, heat_z), f32),
            vmem((heat_x + 2, heat_y, heat_z), f32),
            vmem((heat_x + 2, heat_y, heat_z), f32),
            vmem(heat_mat.shape, jnp.int32),
            vmem((heat_x + 2, heat_y, heat_z), f32),
            vmem((7, heat_x, heat_y, heat_z), f32),
            vmem((heat_x, heat_y, heat_z), f32),
            vmem((2, 2, 2, size_x, 1, size_z), f32),
            vmem((2, 2, 2, size_x, 1, size_z), f32),
            vmem((2, 2, 2, size_x * size_y // LANES, 1, LANES), f32),
            vmem((2, 2, 2, size_x * size_y // LANES, 1, LANES), f32),
            vmem((4, 2, heat_x, 1, heat_z), f32),
            vmem((4, 2, heat_x, 1, heat_z), f32),
            vmem((4, 2, heat_x * heat_y // LANES, 1, LANES), f32),
            vmem((4, 2, heat_x * heat_y // LANES, 1, LANES), f32),
            vmem((2 * size_z, size_x * size_y), bf16),
            vmem((size_x * size_y, n_gy * LANES), bf16),
            vmem((group, 1, LANES), f32),
            vmem((group, 1, LANES), f32),
            vmem((heat_x * heat_y, per * LANES), bf16),
            vmem((heat_z, per * LANES), bf16),
            vmem((heat_z, per * LANES), bf16),
            vmem((heat_x * heat_y, heat_z), f32),
            pltpu.SemaphoreType.DMA((10,)),
            pltpu.SemaphoreType.DMA((6, 6)),
            pltpu.SemaphoreType.DMA((6, 6)),
            pltpu.SemaphoreType.DMA,
            pltpu.SemaphoreType.DMA((n_gx,)),
        ],
        compiler_params=pltpu.CompilerParams(
            collective_id=0, has_side_effects=True, vmem_limit_bytes=56 << 20
        ),
    )(vec_prev, source, mag_mat, send_idx, send_count, recv_cell, temp, heat_mat)


def solution(mesh):
    placed = (
        P(None, "gx", "gy", "gz"),
        P(None, "gx", "gy", "gz"),
        P("gx", "gy", "gz"),
        P(("gx", "gy", "gz"), None, None),
        P(("gx", "gy", "gz"), None),
        P(("gx", "gy", "gz"), None, None),
        P("gx", "gy", "gz"),
        P("gx", "gy", "gz"),
    )
    return jax.shard_map(
        shards,
        mesh=mesh,
        in_specs=placed,
        out_specs=(P(None, "gx", "gy", "gz"), P("gx", "gy", "gz")),
        check_vma=False,
    )
```

```python
import jax
import jax.numpy as jnp
from jax import lax
from jax.experimental import pallas as pl
from jax.experimental.pallas import tpu as pltpu
from jax.sharding import PartitionSpec as P

sigma_table = (0.0, 3.0, 1.5, 6.0)
conduct_table = (1.0, 0.15, 0.05, 0.9)
capacity_table = (7.0, 2.0, 1.0, 6.0)
upwind_rate = 0.3
real_table = tuple(6.0 / (36.0 + s * s) for s in sigma_table)
imag_table = tuple(s / (36.0 + s * s) for s in sigma_table)
inverse_capacity = tuple(1.0 / c for c in capacity_table)

MESH = pl.DeviceIdType.MESH
LANES = 128
AXES = ("gx", "gy", "gz")
f32 = jnp.float32
bf16 = jnp.bfloat16


def lookup(material, table):
    first = jnp.where(material == 0, f32(table[0]), f32(table[1]))
    second = jnp.where(material == 2, f32(table[2]), f32(table[3]))
    return jnp.where(material < 2, first, second)


def halves(value):
    high = value.astype(bf16)
    return high, (value - high.astype(f32)).astype(bf16)


class Exchange:
    def __init__(self, number, sends, receives, faces):
        self.number, self.sends, self.receives, self.faces = number, sends, receives, faces

    def each(self):
        for at, (axis, (low_face, high_face), (low_halo, high_halo)) in enumerate(self.faces):
            me, count = lax.axis_index(axis), lax.axis_size(axis)
            up = pltpu.make_async_remote_copy(
                src_ref=high_face, dst_ref=low_halo,
                send_sem=self.sends.at[self.number, 2 * at],
                recv_sem=self.receives.at[self.number, 2 * at],
                device_id={axis: wrap(me + 1, count)}, device_id_type=MESH,
            )
            down = pltpu.make_async_remote_copy(
                src_ref=low_face, dst_ref=high_halo,
                send_sem=self.sends.at[self.number, 2 * at + 1],
                recv_sem=self.receives.at[self.number, 2 * at + 1],
                device_id={axis: wrap(me + count - 1, count)}, device_id_type=MESH,
            )
            yield me > 0, me < count - 1, up, down, low_halo, high_halo

    def start(self, only=AXES):
        for (axis, _, _), (below, above, up, down, _, _) in zip(self.faces, self.each()):
            if axis in only:
                pl.when(above)(up.start)
                pl.when(below)(down.start)

    def wait(self):
        for below, above, up, down, low_halo, high_halo in self.each():
            pl.when(below)(up.wait_recv)
            pl.when(above)(down.wait_recv)

    def clear(self):
        for axis, _, (low_halo, high_halo) in self.faces:
            me, count = lax.axis_index(axis), lax.axis_size(axis)

            @pl.when(me == 0)
            def _():
                low_halo[...] = jnp.zeros(low_halo.shape, f32)

            @pl.when(me == count - 1)
            def _():
                high_halo[...] = jnp.zeros(high_halo.shape, f32)

    def drain(self):
        for below, above, up, down, _, _ in self.each():
            pl.when(above)(up.wait_send)
            pl.when(below)(down.wait_send)


def iota(shape, dim):
    return lax.broadcasted_iota(jnp.int32, shape, dim)


def wrap(value, count):
    return value & (count - 1) if count & (count - 1) == 0 else lax.rem(value, count)


def face_columns(planes):
    stacked = jnp.concatenate(planes, axis=0)
    depth = stacked.shape[1]
    low = jnp.transpose(stacked[:, :LANES])
    high = low if depth == LANES else jnp.transpose(stacked[:, depth - LANES:])
    return low[0:1, :], high[LANES - 1:LANES, :]


def halo_columns(low, high):
    sub = iota((LANES, LANES), 0)
    return jnp.transpose(jnp.where(sub == 0, low, jnp.where(sub == LANES - 1, high, f32(0.0))))


def column_shifts(plane, halo):
    rows, depth = plane.shape
    lane = iota((rows, depth), 1)
    if depth > LANES and halo.ndim:
        halo = jnp.concatenate([halo] * (depth // LANES), axis=1)
    return (
        jnp.where(lane == 0, halo, pltpu.roll(plane, 1, 1)),
        jnp.where(lane == depth - 1, halo, pltpu.roll(plane, depth - 1, 1)),
    )


def row_shifts(plane, low, high):
    rows, depth = plane.shape
    row = iota((rows, depth), 0)
    return (
        jnp.where(row == 0, low, pltpu.roll(plane, 1, 0)),
        jnp.where(row == rows - 1, high, pltpu.roll(plane, rows - 1, 0)),
    )


def kernel(
    vec_hbm, source_hbm, mag_hbm, idx_hbm, count_hbm, cell_hbm, temp_hbm, heat_hbm,
    potential_hbm, out_hbm,
    field0, field1, source, mag, idx, count_ref, cell, temp0, temp1, temp2, heat_mat, kcell, coef, rate,
    near, xh_m, ys_m, yh_m, zs_m, zh_m, xh_t, partial, ys_t, yh_t, zs_t, zh_t,
    table, chosen, sent, landed, one_hot, v_high, v_low, heat,
    load_sems, halo_send, halo_recv, slot_send, slot_recv,
):
    _, size_x, size_y, size_z = source.shape
    heat_x, heat_y, heat_z = heat_mat.shape
    n_gx, n_gy = lax.axis_size("gx"), lax.axis_size("gy")
    ix, iy, iz, n_gz = lax.axis_index("gx"), lax.axis_index("gy"), lax.axis_index("gz"), lax.axis_size("gz")
    group, here = n_gx * n_gy, ix * n_gy + iy

    loads = [
        pltpu.make_async_copy(src, dst, load_sems.at[at])
        for at, (src, dst) in enumerate(
            [
                (vec_hbm, field0.at[:, pl.ds(1, size_x)]),
                (temp_hbm, temp0.at[pl.ds(1, heat_x)]),
                (heat_hbm, heat_mat),
                (mag_hbm, mag),
                (source_hbm, source),
                (idx_hbm.at[0], idx),
                (cell_hbm.at[0], cell),
                (count_hbm, count_ref),
            ]
        )
    ]
    for load in loads:
        load.start()

    barrier = pltpu.get_barrier_semaphore()

    def greet(device):
        pl.semaphore_signal(barrier, inc=1, device_id=device, device_id_type=MESH)

    for step in range(1, n_gy):
        greet({"gy": wrap(iy + step, n_gy)})

    @pl.loop(1, n_gx)
    def _(step):
        for other in range(n_gy):
            greet({"gx": wrap(ix + step, n_gx), "gy": other})

    @pl.when(iz > 0)
    def _():
        greet({"gz": wrap(iz + n_gz - 1, n_gz)})

    @pl.when(iz < n_gz - 1)
    def _():
        greet({"gz": wrap(iz + 1, n_gz)})

    def faces(x_low, x_high, x_low_halo, x_high_halo, ys, yh, zs, zh, at):
        return [
            ("gx", (x_low, x_high), (x_low_halo, x_high_halo)),
            ("gy", (ys.at[at, 0], ys.at[at, 1]), (yh.at[at, 0], yh.at[at, 1])),
            ("gz", (zs.at[at, 0], zs.at[at, 1]), (zh.at[at, 0], zh.at[at, 1])),
        ]

    def mag_round(number, field):
        return Exchange(
            number, halo_send, halo_recv,
            faces(
                field.at[:, 1], field.at[:, size_x], xh_m.at[number, 0], xh_m.at[number, 1],
                ys_m, yh_m, zs_m, zh_m, number,
            ),
        )

    def heat_round(number, at, state):
        return Exchange(
            number, halo_send, halo_recv,
            faces(
                state.at[1], state.at[heat_x], xh_t.at[at, 0], xh_t.at[at, 1],
                ys_t, yh_t, zs_t, zh_t, at,
            ),
        )

    round0 = mag_round(0, field0)
    round1 = mag_round(1, field1)
    round_t = heat_round(2, 0, temp0)
    round_k = heat_round(3, 1, kcell)
    round_1 = heat_round(4, 2, temp1)
    round_2 = heat_round(5, 3, temp2)
    rounds = (round0, round1, round_t, round_k, round_1, round_2)
    for each in rounds:
        each.clear()
    for field in (field0, field1):
        for x in (0, size_x + 1):
            field[:, x] = jnp.zeros((2, size_y, size_z), f32)
    for state in (temp1, temp2):
        for x in (0, heat_x + 1):
            state[x] = jnp.zeros((heat_y, heat_z), f32)

    block = LANES // size_y
    block_t = LANES // heat_y

    def pack_rows(at, j, part, planes):
        for i, plane in enumerate(planes):
            ys_m[at, 0, part, j * block + i] = plane[0:1, :]
            ys_m[at, 1, part, j * block + i] = plane[size_y - 1:size_y, :]

    def pack_columns(at, field):
        @pl.loop(0, size_x // block)
        def _(j):
            for part in range(2):
                planes = [field[part, j * block + i + 1] for i in range(block)]
                zs_m[at, 0, part, j], zs_m[at, 1, part, j] = face_columns(planes)

    def pack_heat(at, j, planes):
        for i, plane in enumerate(planes):
            ys_t[at, 0, j * block_t + i] = plane[0:1, :]
            ys_t[at, 1, j * block_t + i] = plane[heat_y - 1:heat_y, :]
        zs_t[at, 0, j], zs_t[at, 1, j] = face_columns(planes)

    loads[0].wait()

    @pl.loop(0, size_x // block)
    def _(j):
        for part in range(2):
            pack_rows(0, j, part, [field0[part, j * block + i + 1] for i in range(block)])

    pl.semaphore_wait(barrier, group - 1 + (iz > 0).astype(jnp.int32) + (iz < n_gz - 1).astype(jnp.int32))
    round0.start(("gx", "gy"))
    pack_columns(0, field0)
    round0.start(("gz",))

    loads[1].wait()
    loads[2].wait()

    @pl.loop(0, heat_x // block_t)
    def _(j):
        planes = []
        for i in range(block_t):
            x = j * block_t + i
            planes.append(lookup(heat_mat[x], conduct_table))
            kcell[x + 1] = planes[-1]
        pack_heat(1, j, planes)
        pack_heat(0, j, [temp0[j * block_t + i + 1] for i in range(block_t)])

    round_t.start()
    round_k.start()

    def add_near(field):
        @pl.loop(0, size_x // block)
        def _(j):
            for part in range(2):
                for i in range(block):
                    x = j * block + i
                    plane = field[part, x + 1]
                    low_y, high_y = row_shifts(plane, f32(0.0), f32(0.0))
                    low_z, high_z = column_shifts(plane, f32(0.0))
                    near[part, x] = (field[part, x] + field[part, x + 2]) + (low_y + high_y) + (low_z + high_z)

    add_near(field0)
    for load in loads[3:]:
        load.wait()

    row_m = iota((size_y, size_z), 0)

    def add_planes(at):
        for part in range(2):
            near[part, 0] += xh_m[at, 0, part]
            near[part, size_x - 1] += xh_m[at, 1, part]

    def relaxed(at, j):
        columns = [halo_columns(zh_m[at, 0, part, j], zh_m[at, 1, part, j]) for part in range(2)]
        result = ([], [])
        for i in range(block):
            x = j * block + i
            total = []
            for part in range(2):
                rows = jnp.where(
                    row_m == 0, yh_m[at, 0, part, x], jnp.where(row_m == size_y - 1, yh_m[at, 1, part, x], f32(0.0))
                )
                total.append(
                    (source[part, x] + near[part, x]) + (rows + columns[part][i * size_y:(i + 1) * size_y, :])
                )
            material = mag[x]
            real, imag = lookup(material, real_table), lookup(material, imag_table)
            result[0].append(real * total[0] + imag * total[1])
            result[1].append(real * total[1] - imag * total[0])
        return result

    round0.wait()
    add_planes(0)

    @pl.loop(0, size_x // block)
    def _(j):
        for part, planes in enumerate(relaxed(0, j)):
            for i, plane in enumerate(planes):
                field1[part, j * block + i + 1] = plane
            pack_rows(1, j, part, planes)

    round1.start(("gx", "gy"))
    pack_columns(1, field1)
    round1.start(("gz",))

    round_t.wait()
    round_k.wait()
    for at, state in enumerate((temp0, kcell)):
        state[0] = xh_t[at, 0]
        state[heat_x + 1] = xh_t[at, 1]

    def neighbours(at, state, j):
        columns = halo_columns(zh_t[at, 0, j], zh_t[at, 1, j])
        for i in range(block_t):
            x = j * block_t + i
            plane = state[x + 1]
            low_y, high_y = row_shifts(plane, yh_t[at, 0, x], yh_t[at, 1, x])
            low_z, high_z = column_shifts(plane, columns[i * heat_y:(i + 1) * heat_y, :])
            yield x, plane, (state[x], state[x + 2], low_y, high_y, low_z, high_z)

    @pl.loop(0, heat_x // block_t)
    def _(j):
        for (x, conduct, beside), (_, plane, around) in zip(neighbours(1, kcell, j), neighbours(0, temp0, j)):
            material = heat_mat[x]
            inverse = lookup(material, inverse_capacity)
            upwind = jnp.where(material == 1, f32(upwind_rate), f32(0.0))
            twice = (2.0 * inverse) * conduct
            centre = 1.0 - upwind
            total = jnp.zeros(plane.shape, f32)
            for side in range(6):
                weight = twice * beside[side] / (conduct + beside[side])
                centre = centre - weight
                if side == 4:
                    weight = weight + upwind
                coef[side, x] = weight
                total = total + weight * around[side]
            coef[6, x] = centre
            rate[x] = inverse
            temp1[x + 1] = total + centre * plane

    add_near(field1)
    round1.wait()
    add_planes(1)
    round0.drain()

    @pl.loop(0, size_x // block)
    def _(j):
        losses = []
        for i, planes in enumerate(zip(*relaxed(1, j))):
            x = j * block + i
            field0[0, x + 1] = planes[0]
            field0[1, x + 1] = planes[1]
            losses.append(
                (0.5 * lookup(mag[x], sigma_table)) * (planes[0] * planes[0] + planes[1] * planes[1])
            )
        high, low = halves(jnp.transpose(jnp.concatenate(losses, axis=0)))
        at = pl.ds(pl.multiple_of(j * LANES, LANES), LANES)
        table[0:size_z, at] = high
        table[size_z:2 * size_z, at] = low

    store_potential = pltpu.make_async_copy(
        field0.at[:, pl.ds(1, size_x)], potential_hbm, load_sems.at[8]
    )
    store_potential.start()

    table_rows = size_x * size_y
    targets = chosen.shape[1] // LANES // n_gy
    slot = iota((1, LANES), 1)
    row16 = lax.broadcasted_iota(jnp.int16, (table_rows, LANES), 0)
    sub_z = iota((size_z, LANES), 0)

    def slot_copy(gx, gy):
        return pltpu.make_async_remote_copy(
            src_ref=sent.at[gx * n_gy + gy], dst_ref=landed.at[here],
            send_sem=slot_send, recv_sem=slot_recv.at[ix],
            device_id={"gx": gx, "gy": gy}, device_id_type=MESH,
        )

    def slots_from(gx, count):
        rows = landed.at[pl.ds(gx * n_gy, count)]
        return pltpu.make_async_remote_copy(
            src_ref=rows, dst_ref=rows, send_sem=slot_send, recv_sem=slot_recv.at[gx],
            device_id={"gx": wrap(ix + 1, n_gx)}, device_id_type=MESH,
        )

    @pl.loop(0, n_gx // targets)
    def _(step):
        peers = []
        for k in range(targets):
            target = wrap(ix + step * targets + k + 1, n_gx)
            peers += [(target, gy, target * n_gy + gy) for gy in range(n_gy)]
        cells = []
        for p, (_, _, peer) in enumerate(peers):
            wanted = jnp.where(slot < count_ref[0, peer], idx[pl.ds(peer, 1), :], -1)
            cells.append(wanted)
            row = jnp.broadcast_to(lax.shift_right_arithmetic(wanted, 7).astype(jnp.int16), (table_rows, LANES))
            chosen[:, LANES * p:LANES * (p + 1)] = jnp.where(row16 == row, jnp.ones((), bf16), jnp.zeros((), bf16))
        found = jnp.dot(table[...], chosen[...], preferred_element_type=f32)
        found = found[:size_z] + found[size_z:]
        for p, (target, gy, peer) in enumerate(peers):
            hit = sub_z == (cells[p] & (size_z - 1))
            sent[peer] = jnp.sum(
                jnp.where(hit, found[:, LANES * p:LANES * (p + 1)], 0.0), axis=0, keepdims=True
            )

            @pl.when(peer != here)
            def _():
                slot_copy(target, gy).start()

    landed[here] = sent[here]

    row_h = lax.broadcasted_iota(jnp.int16, (heat_x * heat_y, LANES), 0)
    row_z = lax.broadcasted_iota(jnp.int16, (heat_z, LANES), 0)
    shift = heat_z.bit_length() - 1
    heat[...] = jnp.zeros(heat.shape, f32)
    per = one_hot.shape[1] // LANES // n_gy
    zero16 = jnp.zeros((), bf16)
    transposed = (((1,), (1,)), ((), ()))

    @pl.loop(0, n_gx // per)
    def _(step):
        peers = []
        for k in range(per):
            gx = wrap(ix + 2 * n_gx - 1 - (step * per + k), n_gx)

            @pl.when(gx != ix)
            def _():
                slots_from(gx, n_gy).wait_recv()

            @pl.when(gx == ix)
            def _():
                slots_from(gx, n_gy - 1).wait_recv()

            peers += [gx * n_gy + gy for gy in range(n_gy)]

        for p, peer in enumerate(peers):
            target = cell[pl.ds(peer, 1), :]
            high, low = halves(landed[peer])
            at = slice(LANES * p, LANES * (p + 1))
            row = jnp.broadcast_to(lax.shift_right_logical(target, shift).astype(jnp.int16), row_h.shape)
            one_hot[:, at] = jnp.where(row_h == row, jnp.ones((), bf16), zero16)
            hit = row_z == jnp.broadcast_to((target & (heat_z - 1)).astype(jnp.int16), row_z.shape)
            v_high[:, at] = jnp.where(hit, jnp.broadcast_to(high, row_z.shape), zero16)
            v_low[:, at] = jnp.where(hit, jnp.broadcast_to(low, row_z.shape), zero16)
        heat[...] += lax.dot_general(
            one_hot[...], v_high[...], transposed, preferred_element_type=f32
        ) + lax.dot_general(one_hot[...], v_low[...], transposed, preferred_element_type=f32)

    @pl.loop(0, heat_x // block_t)
    def _(j):
        planes = []
        for i in range(block_t):
            x = j * block_t + i
            gain = heat[pl.ds(pl.multiple_of(x * heat_y, heat_y), heat_y), :] * rate[x]
            rate[x] = gain
            planes.append(temp1[x + 1] + gain)
            temp1[x + 1] = planes[-1]
        pack_heat(2, j, planes)

    round_1.start()
    round_t.drain()

    row_t = iota((heat_y, heat_z), 0)
    depth_t = iota((heat_y, heat_z), 1)

    def step_near(state):
        @pl.loop(0, heat_x // block_t)
        def _(j):
            for i in range(block_t):
                x = j * block_t + i
                plane = state[x + 1]
                around = (
                    (state[x], state[x + 2])
                    + row_shifts(plane, f32(0.0), f32(0.0))
                    + column_shifts(plane, f32(0.0))
                )
                total = coef[6, x] * plane + rate[x]
                for side, other in enumerate(around):
                    total = total + coef[side, x] * other
                partial[x] = total

    def add_ends(at):
        partial[0] += coef[0, 0] * xh_t[at, 0]
        partial[heat_x - 1] += coef[1, heat_x - 1] * xh_t[at, 1]

    def stepped(at, j):
        columns = halo_columns(zh_t[at, 0, j], zh_t[at, 1, j])
        columns = jnp.concatenate([columns] * (heat_z // LANES), axis=1)
        for i in range(block_t):
            x = j * block_t + i
            column = columns[i * heat_y:(i + 1) * heat_y, :]
            low_y, high_y = coef[2, x] * yh_t[at, 0, x], coef[3, x] * yh_t[at, 1, x]
            low_z, high_z = coef[4, x] * column, coef[5, x] * column
            zero = f32(0.0)
            rows = jnp.where(row_t == 0, low_y, jnp.where(row_t == heat_y - 1, high_y, zero))
            ends = jnp.where(depth_t == 0, low_z, jnp.where(depth_t == heat_z - 1, high_z, zero))
            yield x, partial[x] + (rows + ends)

    step_near(temp1)
    round_1.wait()
    add_ends(2)

    @pl.loop(0, heat_x // block_t)
    def _(j):
        planes = []
        for x, plane in stepped(2, j):
            temp2[x + 1] = plane
            planes.append(plane)
        pack_heat(3, j, planes)

    round_2.start()
    step_near(temp2)
    round_2.wait()
    add_ends(3)

    @pl.loop(0, heat_x // block_t)
    def _(j):
        for x, plane in stepped(3, j):
            temp0[x + 1] = plane

    store_temp = pltpu.make_async_copy(temp0.at[pl.ds(1, heat_x)], out_hbm, load_sems.at[9])
    store_temp.start()
    for each in (round1, round_k, round_1, round_2):
        each.drain()

    everyone = sent.at[pl.ds(0, group - 1)]
    pltpu.make_async_remote_copy(
        src_ref=everyone, dst_ref=everyone, send_sem=slot_send, recv_sem=slot_recv.at[0],
        device_id={"gx": wrap(ix + 1, n_gx)}, device_id_type=MESH,
    ).wait_send()
    store_potential.wait()
    store_temp.wait()


def finish(potential_in, temp_in, potential_out, temp_out, potential, temp, sems):
    pieces = 4
    size_x = potential.shape[1] // pieces
    steps = []
    for piece in range(pieces):
        at = pl.ds(piece * size_x, size_x)
        steps.append((potential_in.at[:, at], potential.at[:, at], potential_out.at[:, at]))
    steps.append((temp_in, temp, temp_out))
    arrive = [pltpu.make_async_copy(a, b, sems.at[0, k]) for k, (a, b, _) in enumerate(steps)]
    leave = [pltpu.make_async_copy(b, c, sems.at[1, k]) for k, (_, b, c) in enumerate(steps)]
    for copy in arrive:
        copy.start()
    for copy, out in zip(arrive, leave):
        copy.wait()
        out.start()
    for out in leave:
        out.wait()


def shards(vec_prev, source, mag_mat, send_idx, send_count, recv_cell, temp, heat_mat):
    _, size_x, size_y, size_z = vec_prev.shape
    heat_x, heat_y, heat_z = temp.shape
    n_gx, n_gy = lax.axis_size("gx"), lax.axis_size("gy")
    group = n_gx * n_gy
    per = max(1, n_gx // 2) * n_gy
    vmem = pltpu.VMEM
    anywhere = pl.BlockSpec(memory_space=pl.ANY)
    results = pl.pallas_call(
        kernel,
        out_shape=(
            jax.ShapeDtypeStruct(vec_prev.shape, f32),
            jax.ShapeDtypeStruct(temp.shape, f32),
        ),
        in_specs=[anywhere] * 8,
        out_specs=(anywhere, anywhere),
        scratch_shapes=[
            vmem((2, size_x + 2, size_y, size_z), f32),
            vmem((2, size_x + 2, size_y, size_z), f32),
            vmem(source.shape, f32),
            vmem(mag_mat.shape, jnp.int32),
            vmem(send_idx.shape[1:], jnp.int32),
            pltpu.SMEM(send_count.shape, jnp.int32),
            vmem(recv_cell.shape[1:], jnp.int32),
            vmem((heat_x + 2, heat_y, heat_z), f32),
            vmem((heat_x + 2, heat_y, heat_z), f32),
            vmem((heat_x + 2, heat_y, heat_z), f32),
            vmem(heat_mat.shape, jnp.int32),
            vmem((heat_x + 2, heat_y, heat_z), f32),
            vmem((7, heat_x, heat_y, heat_z), f32),
            vmem((heat_x, heat_y, heat_z), f32),
            vmem(source.shape, f32),
            vmem((2, 2, 2, size_y, size_z), f32),
            vmem((2, 2, 2, size_x, 1, size_z), f32),
            vmem((2, 2, 2, size_x, 1, size_z), f32),
            vmem((2, 2, 2, size_x * size_y // LANES, 1, LANES), f32),
            vmem((2, 2, 2, size_x * size_y // LANES, 1, LANES), f32),
            vmem((4, 2, heat_y, heat_z), f32),
            vmem((heat_x, heat_y, heat_z), f32),
            vmem((4, 2, heat_x, 1, heat_z), f32),
            vmem((4, 2, heat_x, 1, heat_z), f32),
            vmem((4, 2, heat_x * heat_y // LANES, 1, LANES), f32),
            vmem((4, 2, heat_x * heat_y // LANES, 1, LANES), f32),
            vmem((2 * size_z, size_x * size_y), bf16),
            vmem((size_x * size_y, per * LANES), bf16),
            vmem((group, 1, LANES), f32),
            vmem((group, 1, LANES), f32),
            vmem((heat_x * heat_y, per * LANES), bf16),
            vmem((heat_z, per * LANES), bf16),
            vmem((heat_z, per * LANES), bf16),
            vmem((heat_x * heat_y, heat_z), f32),
            pltpu.SemaphoreType.DMA((10,)),
            pltpu.SemaphoreType.DMA((6, 6)),
            pltpu.SemaphoreType.DMA((6, 6)),
            pltpu.SemaphoreType.DMA,
            pltpu.SemaphoreType.DMA((n_gx,)),
        ],
        compiler_params=pltpu.CompilerParams(
            collective_id=0, has_side_effects=True, vmem_limit_bytes=60 << 20
        ),
    )(vec_prev, source, mag_mat, send_idx, send_count, recv_cell, temp, heat_mat)
    return pl.pallas_call(
        finish,
        out_shape=tuple(jax.ShapeDtypeStruct(result.shape, f32) for result in results),
        in_specs=[anywhere] * 2,
        out_specs=(anywhere, anywhere),
        scratch_shapes=[
            vmem(vec_prev.shape, f32),
            vmem(temp.shape, f32),
            pltpu.SemaphoreType.DMA((2, 5)),
        ],
        compiler_params=pltpu.CompilerParams(vmem_limit_bytes=60 << 20),
    )(*results)


def solution(mesh):
    placed = (
        P(None, "gx", "gy", "gz"),
        P(None, "gx", "gy", "gz"),
        P("gx", "gy", "gz"),
        P(("gx", "gy", "gz"), None, None),
        P(("gx", "gy", "gz"), None),
        P(("gx", "gy", "gz"), None, None),
        P("gx", "gy", "gz"),
        P("gx", "gy", "gz"),
    )
    return jax.shard_map(
        shards,
        mesh=mesh,
        in_specs=placed,
        out_specs=(P(None, "gx", "gy", "gz"), P("gx", "gy", "gz")),
        check_vma=False,
    )
```

```python
import jax
import jax.numpy as jnp
from jax import lax
from jax.experimental import pallas as pl
from jax.experimental.pallas import tpu as pltpu
from jax.sharding import PartitionSpec as P

sigma_table = (0.0, 3.0, 1.5, 6.0)
conduct_table = (1.0, 0.15, 0.05, 0.9)
capacity_table = (7.0, 2.0, 1.0, 6.0)
upwind_rate = 0.3
real_table = tuple(6.0 / (36.0 + s * s) for s in sigma_table)
imag_table = tuple(s / (36.0 + s * s) for s in sigma_table)
inverse_capacity = tuple(1.0 / c for c in capacity_table)

MESH = pl.DeviceIdType.MESH
LANES = 128
AXES = ("gx", "gy", "gz")
f32 = jnp.float32
bf16 = jnp.bfloat16


def lookup(material, table):
    first = jnp.where(material == 0, f32(table[0]), f32(table[1]))
    second = jnp.where(material == 2, f32(table[2]), f32(table[3]))
    return jnp.where(material < 2, first, second)


def halves(value):
    high = value.astype(bf16)
    return high, (value - high.astype(f32)).astype(bf16)


class Exchange:
    def __init__(self, number, sends, receives, faces):
        self.number, self.sends, self.receives, self.faces = number, sends, receives, faces

    def each(self):
        for at, (axis, (low_face, high_face), (low_halo, high_halo)) in enumerate(self.faces):
            me, count = lax.axis_index(axis), lax.axis_size(axis)
            up = pltpu.make_async_remote_copy(
                src_ref=high_face, dst_ref=low_halo,
                send_sem=self.sends.at[self.number, 2 * at],
                recv_sem=self.receives.at[self.number, 2 * at],
                device_id={axis: wrap(me + 1, count)}, device_id_type=MESH,
            )
            down = pltpu.make_async_remote_copy(
                src_ref=low_face, dst_ref=high_halo,
                send_sem=self.sends.at[self.number, 2 * at + 1],
                recv_sem=self.receives.at[self.number, 2 * at + 1],
                device_id={axis: wrap(me + count - 1, count)}, device_id_type=MESH,
            )
            yield me > 0, me < count - 1, up, down, low_halo, high_halo

    def start(self, only=AXES):
        for (axis, _, _), (below, above, up, down, _, _) in zip(self.faces, self.each()):
            if axis in only:
                pl.when(above)(up.start)
                pl.when(below)(down.start)

    def wait(self):
        for below, above, up, down, low_halo, high_halo in self.each():
            pl.when(below)(up.wait_recv)
            pl.when(above)(down.wait_recv)

    def clear(self):
        for axis, _, (low_halo, high_halo) in self.faces:
            me, count = lax.axis_index(axis), lax.axis_size(axis)

            @pl.when(me == 0)
            def _():
                low_halo[...] = jnp.zeros(low_halo.shape, f32)

            @pl.when(me == count - 1)
            def _():
                high_halo[...] = jnp.zeros(high_halo.shape, f32)

    def drain(self):
        for below, above, up, down, _, _ in self.each():
            pl.when(above)(up.wait_send)
            pl.when(below)(down.wait_send)


def iota(shape, dim):
    return lax.broadcasted_iota(jnp.int32, shape, dim)


def wrap(value, count):
    return value & (count - 1) if count & (count - 1) == 0 else lax.rem(value, count)


def face_columns(planes):
    stacked = jnp.concatenate(planes, axis=0)
    depth = stacked.shape[1]
    low = jnp.transpose(stacked[:, :LANES])
    high = low if depth == LANES else jnp.transpose(stacked[:, depth - LANES:])
    return low[0:1, :], high[LANES - 1:LANES, :]


def halo_columns(low, high):
    sub = iota((LANES, LANES), 0)
    return jnp.transpose(jnp.where(sub == 0, low, jnp.where(sub == LANES - 1, high, f32(0.0))))


def column_shifts(plane, halo):
    rows, depth = plane.shape
    lane = iota((rows, depth), 1)
    if depth > LANES and halo.ndim:
        halo = jnp.concatenate([halo] * (depth // LANES), axis=1)
    return (
        jnp.where(lane == 0, halo, pltpu.roll(plane, 1, 1)),
        jnp.where(lane == depth - 1, halo, pltpu.roll(plane, depth - 1, 1)),
    )


def row_shifts(plane, low, high):
    rows, depth = plane.shape
    row = iota((rows, depth), 0)
    return (
        jnp.where(row == 0, low, pltpu.roll(plane, 1, 0)),
        jnp.where(row == rows - 1, high, pltpu.roll(plane, rows - 1, 0)),
    )


def kernel(
    vec_hbm, source_hbm, mag_hbm, idx_hbm, count_hbm, cell_hbm, temp_hbm, heat_hbm,
    potential_hbm, out_hbm,
    field0, field1, source, mag, idx, count_ref, cell, temp0, temp1, temp2, heat_mat, kcell, coef, rate,
    near, xh_m, ys_m, yh_m, zs_m, zh_m, xh_t, partial, ys_t, yh_t, zs_t, zh_t,
    table, chosen, sent, landed, one_hot, v_high, v_low, heat,
    load_sems, halo_send, halo_recv, slot_send, slot_recv,
):
    _, size_x, size_y, size_z = source.shape
    heat_x, heat_y, heat_z = heat_mat.shape
    n_gx, n_gy = lax.axis_size("gx"), lax.axis_size("gy")
    ix, iy, iz, n_gz = lax.axis_index("gx"), lax.axis_index("gy"), lax.axis_index("gz"), lax.axis_size("gz")
    group, here = n_gx * n_gy, ix * n_gy + iy

    loads = [
        pltpu.make_async_copy(src, dst, load_sems.at[at])
        for at, (src, dst) in enumerate(
            [
                (vec_hbm, field0.at[:, pl.ds(1, size_x)]),
                (temp_hbm, temp0.at[pl.ds(1, heat_x)]),
                (heat_hbm, heat_mat),
                (mag_hbm, mag),
                (source_hbm, source),
                (idx_hbm.at[0], idx),
                (cell_hbm.at[0], cell),
                (count_hbm, count_ref),
            ]
        )
    ]
    for load in loads:
        load.start()

    barrier = pltpu.get_barrier_semaphore()

    def greet(device):
        pl.semaphore_signal(barrier, inc=1, device_id=device, device_id_type=MESH)

    for step in range(1, n_gy):
        greet({"gy": wrap(iy + step, n_gy)})

    @pl.loop(1, n_gx)
    def _(step):
        for other in range(n_gy):
            greet({"gx": wrap(ix + step, n_gx), "gy": other})

    @pl.when(iz > 0)
    def _():
        greet({"gz": wrap(iz + n_gz - 1, n_gz)})

    @pl.when(iz < n_gz - 1)
    def _():
        greet({"gz": wrap(iz + 1, n_gz)})

    def faces(x_low, x_high, x_low_halo, x_high_halo, ys, yh, zs, zh, at):
        return [
            ("gx", (x_low, x_high), (x_low_halo, x_high_halo)),
            ("gy", (ys.at[at, 0], ys.at[at, 1]), (yh.at[at, 0], yh.at[at, 1])),
            ("gz", (zs.at[at, 0], zs.at[at, 1]), (zh.at[at, 0], zh.at[at, 1])),
        ]

    def mag_round(number, field):
        return Exchange(
            number, halo_send, halo_recv,
            faces(
                field.at[:, 1], field.at[:, size_x], xh_m.at[number, 0], xh_m.at[number, 1],
                ys_m, yh_m, zs_m, zh_m, number,
            ),
        )

    def heat_round(number, at, state):
        return Exchange(
            number, halo_send, halo_recv,
            faces(
                state.at[1], state.at[heat_x], xh_t.at[at, 0], xh_t.at[at, 1],
                ys_t, yh_t, zs_t, zh_t, at,
            ),
        )

    round0 = mag_round(0, field0)
    round1 = mag_round(1, field1)
    round_t = heat_round(2, 0, temp0)
    round_k = heat_round(3, 1, kcell)
    round_1 = heat_round(4, 2, temp1)
    round_2 = heat_round(5, 3, temp2)
    rounds = (round0, round1, round_t, round_k, round_1, round_2)
    for each in rounds:
        each.clear()
    for field in (field0, field1):
        for x in (0, size_x + 1):
            field[:, x] = jnp.zeros((2, size_y, size_z), f32)
    for state in (temp1, temp2):
        for x in (0, heat_x + 1):
            state[x] = jnp.zeros((heat_y, heat_z), f32)

    block = LANES // size_y
    block_t = LANES // heat_y

    def pack_mag(at, j, part, planes):
        for i, plane in enumerate(planes):
            ys_m[at, 0, part, j * block + i] = plane[0:1, :]
            ys_m[at, 1, part, j * block + i] = plane[size_y - 1:size_y, :]
        zs_m[at, 0, part, j], zs_m[at, 1, part, j] = face_columns(planes)

    def pack_heat(at, j, planes):
        for i, plane in enumerate(planes):
            ys_t[at, 0, j * block_t + i] = plane[0:1, :]
            ys_t[at, 1, j * block_t + i] = plane[heat_y - 1:heat_y, :]

    def send_heat(each, at, state):
        each.start(("gx", "gy"))

        @pl.loop(0, heat_x // block_t)
        def _(j):
            planes = [state[j * block_t + i + 1] for i in range(block_t)]
            zs_t[at, 0, j], zs_t[at, 1, j] = face_columns(planes)

        each.start(("gz",))

    loads[0].wait()

    @pl.loop(0, size_x // block)
    def _(j):
        for part in range(2):
            pack_mag(0, j, part, [field0[part, j * block + i + 1] for i in range(block)])

    pl.semaphore_wait(barrier, group - 1 + (iz > 0).astype(jnp.int32) + (iz < n_gz - 1).astype(jnp.int32))
    round0.start()

    loads[1].wait()
    loads[2].wait()

    @pl.loop(0, heat_x // block_t)
    def _(j):
        planes = []
        for i in range(block_t):
            x = j * block_t + i
            planes.append(lookup(heat_mat[x], conduct_table))
            kcell[x + 1] = planes[-1]
        pack_heat(1, j, planes)
        pack_heat(0, j, [temp0[j * block_t + i + 1] for i in range(block_t)])

    send_heat(round_t, 0, temp0)
    send_heat(round_k, 1, kcell)

    def add_near(field):
        @pl.loop(0, size_x // block)
        def _(j):
            for part in range(2):
                for i in range(block):
                    x = j * block + i
                    plane = field[part, x + 1]
                    low_y, high_y = row_shifts(plane, f32(0.0), f32(0.0))
                    low_z, high_z = column_shifts(plane, f32(0.0))
                    near[part, x] = (field[part, x] + field[part, x + 2]) + (low_y + high_y) + (low_z + high_z)

    add_near(field0)
    for load in loads[3:]:
        load.wait()

    row_m = iota((size_y, size_z), 0)

    def add_planes(at):
        for part in range(2):
            near[part, 0] += xh_m[at, 0, part]
            near[part, size_x - 1] += xh_m[at, 1, part]

    def relaxed(at, j):
        columns = [halo_columns(zh_m[at, 0, part, j], zh_m[at, 1, part, j]) for part in range(2)]
        result = ([], [])
        for i in range(block):
            x = j * block + i
            total = []
            for part in range(2):
                rows = jnp.where(
                    row_m == 0, yh_m[at, 0, part, x], jnp.where(row_m == size_y - 1, yh_m[at, 1, part, x], f32(0.0))
                )
                total.append(
                    (source[part, x] + near[part, x]) + (rows + columns[part][i * size_y:(i + 1) * size_y, :])
                )
            material = mag[x]
            real, imag = lookup(material, real_table), lookup(material, imag_table)
            result[0].append(real * total[0] + imag * total[1])
            result[1].append(real * total[1] - imag * total[0])
        return result

    round0.wait()
    add_planes(0)

    @pl.loop(0, size_x // block)
    def _(j):
        for part, planes in enumerate(relaxed(0, j)):
            for i, plane in enumerate(planes):
                field1[part, j * block + i + 1] = plane
            pack_mag(1, j, part, planes)

    round1.start()

    round_t.wait()
    round_k.wait()
    for at, state in enumerate((temp0, kcell)):
        state[0] = xh_t[at, 0]
        state[heat_x + 1] = xh_t[at, 1]

    def neighbours(at, state, j):
        columns = halo_columns(zh_t[at, 0, j], zh_t[at, 1, j])
        for i in range(block_t):
            x = j * block_t + i
            plane = state[x + 1]
            low_y, high_y = row_shifts(plane, yh_t[at, 0, x], yh_t[at, 1, x])
            low_z, high_z = column_shifts(plane, columns[i * heat_y:(i + 1) * heat_y, :])
            yield x, plane, (state[x], state[x + 2], low_y, high_y, low_z, high_z)

    @pl.loop(0, heat_x // block_t)
    def _(j):
        for (x, conduct, beside), (_, plane, around) in zip(neighbours(1, kcell, j), neighbours(0, temp0, j)):
            material = heat_mat[x]
            inverse = lookup(material, inverse_capacity)
            upwind = jnp.where(material == 1, f32(upwind_rate), f32(0.0))
            twice = (2.0 * inverse) * conduct
            centre = 1.0 - upwind
            total = jnp.zeros(plane.shape, f32)
            for side in range(6):
                weight = twice * beside[side] / (conduct + beside[side])
                centre = centre - weight
                if side == 4:
                    weight = weight + upwind
                coef[side, x] = weight
                total = total + weight * around[side]
            coef[6, x] = centre
            rate[x] = inverse
            temp1[x + 1] = total + centre * plane

    add_near(field1)
    round1.wait()
    add_planes(1)
    round0.drain()

    @pl.loop(0, size_x // block)
    def _(j):
        losses = []
        for i, planes in enumerate(zip(*relaxed(1, j))):
            x = j * block + i
            field0[0, x + 1] = planes[0]
            field0[1, x + 1] = planes[1]
            losses.append(
                (0.5 * lookup(mag[x], sigma_table)) * (planes[0] * planes[0] + planes[1] * planes[1])
            )
        high, low = halves(jnp.transpose(jnp.concatenate(losses, axis=0)))
        at = pl.ds(pl.multiple_of(j * LANES, LANES), LANES)
        table[0:size_z, at] = high
        table[size_z:2 * size_z, at] = low

    store_potential = pltpu.make_async_copy(
        field0.at[:, pl.ds(1, size_x)], potential_hbm, load_sems.at[8]
    )
    store_potential.start()

    table_rows = size_x * size_y
    width = n_gy * LANES
    slot = iota((1, LANES), 1)
    row16 = lax.broadcasted_iota(jnp.int16, (table_rows, LANES), 0)
    sub_z = iota((size_z, LANES), 0)

    def slot_copy(gx, gy):
        return pltpu.make_async_remote_copy(
            src_ref=sent.at[gx * n_gy + gy], dst_ref=landed.at[here],
            send_sem=slot_send, recv_sem=slot_recv.at[ix],
            device_id={"gx": gx, "gy": gy}, device_id_type=MESH,
        )

    def slots_from(gx, count):
        rows = landed.at[pl.ds(gx * n_gy, count)]
        return pltpu.make_async_remote_copy(
            src_ref=rows, dst_ref=rows, send_sem=slot_send, recv_sem=slot_recv.at[gx],
            device_id={"gx": wrap(ix + 1, n_gx)}, device_id_type=MESH,
        )

    @pl.loop(0, n_gx)
    def _(step):
        target = wrap(ix + step + 1, n_gx)
        first = target * n_gy
        cells = []
        for p in range(n_gy):
            wanted = jnp.where(slot < count_ref[0, first + p], idx[pl.ds(first + p, 1), :], -1)
            cells.append(wanted)
            row = jnp.broadcast_to(lax.shift_right_arithmetic(wanted, 7).astype(jnp.int16), (table_rows, LANES))
            chosen[:, LANES * p:LANES * (p + 1)] = jnp.where(row16 == row, jnp.ones((), bf16), jnp.zeros((), bf16))
        found = jnp.dot(table[...], chosen[...], preferred_element_type=f32)
        found = found[:size_z] + found[size_z:]
        for p in range(n_gy):
            hit = sub_z == (cells[p] & (size_z - 1))
            sent[first + p] = jnp.sum(
                jnp.where(hit, found[:, LANES * p:LANES * (p + 1)], 0.0), axis=0, keepdims=True
            )
        for p in range(n_gy):
            @pl.when(first + p != here)
            def _():
                slot_copy(target, p).start()

    landed[here] = sent[here]

    row_h = lax.broadcasted_iota(jnp.int16, (heat_x * heat_y, LANES), 0)
    row_z = lax.broadcasted_iota(jnp.int16, (heat_z, LANES), 0)
    shift = heat_z.bit_length() - 1
    heat[...] = jnp.zeros(heat.shape, f32)
    per = one_hot.shape[1] // LANES // n_gy
    zero16 = jnp.zeros((), bf16)
    transposed = (((1,), (1,)), ((), ()))

    @pl.loop(0, n_gx // per)
    def _(step):
        peers = []
        for k in range(per):
            gx = wrap(ix + 2 * n_gx - 1 - (step * per + k), n_gx)

            @pl.when(gx != ix)
            def _():
                slots_from(gx, n_gy).wait_recv()

            @pl.when(gx == ix)
            def _():
                slots_from(gx, n_gy - 1).wait_recv()

            peers += [gx * n_gy + gy for gy in range(n_gy)]

        for p, peer in enumerate(peers):
            target = cell[pl.ds(peer, 1), :]
            high, low = halves(landed[peer])
            at = slice(LANES * p, LANES * (p + 1))
            row = jnp.broadcast_to(lax.shift_right_logical(target, shift).astype(jnp.int16), row_h.shape)
            one_hot[:, at] = jnp.where(row_h == row, jnp.ones((), bf16), zero16)
            hit = row_z == jnp.broadcast_to((target & (heat_z - 1)).astype(jnp.int16), row_z.shape)
            v_high[:, at] = jnp.where(hit, jnp.broadcast_to(high, row_z.shape), zero16)
            v_low[:, at] = jnp.where(hit, jnp.broadcast_to(low, row_z.shape), zero16)
        heat[...] += lax.dot_general(
            one_hot[...], v_high[...], transposed, preferred_element_type=f32
        ) + lax.dot_general(one_hot[...], v_low[...], transposed, preferred_element_type=f32)

    @pl.loop(0, heat_x // block_t)
    def _(j):
        planes = []
        for i in range(block_t):
            x = j * block_t + i
            gain = heat[pl.ds(pl.multiple_of(x * heat_y, heat_y), heat_y), :] * rate[x]
            rate[x] = gain
            planes.append(temp1[x + 1] + gain)
            temp1[x + 1] = planes[-1]
        pack_heat(2, j, planes)

    send_heat(round_1, 2, temp1)

    row_t = iota((heat_y, heat_z), 0)
    depth_t = iota((heat_y, heat_z), 1)

    def step_near(state):
        @pl.loop(0, heat_x // block_t)
        def _(j):
            for i in range(block_t):
                x = j * block_t + i
                plane = state[x + 1]
                around = (
                    (state[x], state[x + 2])
                    + row_shifts(plane, f32(0.0), f32(0.0))
                    + column_shifts(plane, f32(0.0))
                )
                total = coef[6, x] * plane + rate[x]
                for side, other in enumerate(around):
                    total = total + coef[side, x] * other
                partial[x] = total

    def add_ends(at):
        partial[0] += coef[0, 0] * xh_t[at, 0]
        partial[heat_x - 1] += coef[1, heat_x - 1] * xh_t[at, 1]

    def stepped(at, j):
        columns = halo_columns(zh_t[at, 0, j], zh_t[at, 1, j])
        columns = jnp.concatenate([columns] * (heat_z // LANES), axis=1)
        for i in range(block_t):
            x = j * block_t + i
            column = columns[i * heat_y:(i + 1) * heat_y, :]
            low_y, high_y = coef[2, x] * yh_t[at, 0, x], coef[3, x] * yh_t[at, 1, x]
            low_z, high_z = coef[4, x] * column, coef[5, x] * column
            zero = f32(0.0)
            rows = jnp.where(row_t == 0, low_y, jnp.where(row_t == heat_y - 1, high_y, zero))
            ends = jnp.where(depth_t == 0, low_z, jnp.where(depth_t == heat_z - 1, high_z, zero))
            yield x, partial[x] + (rows + ends)

    step_near(temp1)
    for each in (round1, round_t, round_k):
        each.drain()
    everyone = sent.at[pl.ds(0, group - 1)]
    pltpu.make_async_remote_copy(
        src_ref=everyone, dst_ref=everyone, send_sem=slot_send, recv_sem=slot_recv.at[0],
        device_id={"gx": wrap(ix + 1, n_gx)}, device_id_type=MESH,
    ).wait_send()
    store_potential.wait()
    round_1.wait()
    add_ends(2)

    @pl.loop(0, heat_x // block_t)
    def _(j):
        planes = []
        for x, plane in stepped(2, j):
            temp2[x + 1] = plane
            planes.append(plane)
        pack_heat(3, j, planes)

    send_heat(round_2, 3, temp2)
    step_near(temp2)
    round_1.drain()
    round_2.wait()
    add_ends(3)

    @pl.loop(0, heat_x // block_t)
    def _(j):
        for x, plane in stepped(3, j):
            temp0[x + 1] = plane

    store_temp = pltpu.make_async_copy(temp0.at[pl.ds(1, heat_x)], out_hbm, load_sems.at[9])
    store_temp.start()
    round_2.drain()

    store_temp.wait()


def finish(potential_in, temp_in, potential_out, temp_out, potential, temp, sems):
    pieces = 4
    size_x = potential.shape[1] // pieces
    steps = []
    for piece in range(pieces):
        at = pl.ds(piece * size_x, size_x)
        steps.append((potential_in.at[:, at], potential.at[:, at], potential_out.at[:, at]))
    steps.append((temp_in, temp, temp_out))
    arrive = [pltpu.make_async_copy(a, b, sems.at[0, k]) for k, (a, b, _) in enumerate(steps)]
    leave = [pltpu.make_async_copy(b, c, sems.at[1, k]) for k, (_, b, c) in enumerate(steps)]
    for copy in arrive:
        copy.start()
    for copy, out in zip(arrive, leave):
        copy.wait()
        out.start()
    for out in leave:
        out.wait()


def shards(vec_prev, source, mag_mat, send_idx, send_count, recv_cell, temp, heat_mat):
    _, size_x, size_y, size_z = vec_prev.shape
    heat_x, heat_y, heat_z = temp.shape
    n_gx, n_gy = lax.axis_size("gx"), lax.axis_size("gy")
    group = n_gx * n_gy
    per = min(2, n_gx) * n_gy
    vmem = pltpu.VMEM
    anywhere = pl.BlockSpec(memory_space=pl.ANY)
    results = pl.pallas_call(
        kernel,
        out_shape=(
            jax.ShapeDtypeStruct(vec_prev.shape, f32),
            jax.ShapeDtypeStruct(temp.shape, f32),
        ),
        in_specs=[anywhere] * 8,
        out_specs=(anywhere, anywhere),
        scratch_shapes=[
            vmem((2, size_x + 2, size_y, size_z), f32),
            vmem((2, size_x + 2, size_y, size_z), f32),
            vmem(source.shape, f32),
            vmem(mag_mat.shape, jnp.int32),
            vmem(send_idx.shape[1:], jnp.int32),
            pltpu.SMEM(send_count.shape, jnp.int32),
            vmem(recv_cell.shape[1:], jnp.int32),
            vmem((heat_x + 2, heat_y, heat_z), f32),
            vmem((heat_x + 2, heat_y, heat_z), f32),
            vmem((heat_x + 2, heat_y, heat_z), f32),
            vmem(heat_mat.shape, jnp.int32),
            vmem((heat_x + 2, heat_y, heat_z), f32),
            vmem((7, heat_x, heat_y, heat_z), f32),
            vmem((heat_x, heat_y, heat_z), f32),
            vmem(source.shape, f32),
            vmem((2, 2, 2, size_y, size_z), f32),
            vmem((2, 2, 2, size_x, 1, size_z), f32),
            vmem((2, 2, 2, size_x, 1, size_z), f32),
            vmem((2, 2, 2, size_x * size_y // LANES, 1, LANES), f32),
            vmem((2, 2, 2, size_x * size_y // LANES, 1, LANES), f32),
            vmem((4, 2, heat_y, heat_z), f32),
            vmem((heat_x, heat_y, heat_z), f32),
            vmem((4, 2, heat_x, 1, heat_z), f32),
            vmem((4, 2, heat_x, 1, heat_z), f32),
            vmem((4, 2, heat_x * heat_y // LANES, 1, LANES), f32),
            vmem((4, 2, heat_x * heat_y // LANES, 1, LANES), f32),
            vmem((2 * size_z, size_x * size_y), bf16),
            vmem((size_x * size_y, n_gy * LANES), bf16),
            vmem((group, 1, LANES), f32),
            vmem((group, 1, LANES), f32),
            vmem((heat_x * heat_y, per * LANES), bf16),
            vmem((heat_z, per * LANES), bf16),
            vmem((heat_z, per * LANES), bf16),
            vmem((heat_x * heat_y, heat_z), f32),
            pltpu.SemaphoreType.DMA((10,)),
            pltpu.SemaphoreType.DMA((6, 6)),
            pltpu.SemaphoreType.DMA((6, 6)),
            pltpu.SemaphoreType.DMA,
            pltpu.SemaphoreType.DMA((n_gx,)),
        ],
        compiler_params=pltpu.CompilerParams(
            collective_id=0, has_side_effects=True, vmem_limit_bytes=60 << 20
        ),
    )(vec_prev, source, mag_mat, send_idx, send_count, recv_cell, temp, heat_mat)
    return pl.pallas_call(
        finish,
        out_shape=tuple(jax.ShapeDtypeStruct(result.shape, f32) for result in results),
        in_specs=[anywhere] * 2,
        out_specs=(anywhere, anywhere),
        scratch_shapes=[
            vmem(vec_prev.shape, f32),
            vmem(temp.shape, f32),
            pltpu.SemaphoreType.DMA((2, 5)),
        ],
        compiler_params=pltpu.CompilerParams(vmem_limit_bytes=60 << 20),
    )(*results)


def solution(mesh):
    placed = (
        P(None, "gx", "gy", "gz"),
        P(None, "gx", "gy", "gz"),
        P("gx", "gy", "gz"),
        P(("gx", "gy", "gz"), None, None),
        P(("gx", "gy", "gz"), None),
        P(("gx", "gy", "gz"), None, None),
        P("gx", "gy", "gz"),
        P("gx", "gy", "gz"),
    )
    return jax.shard_map(
        shards,
        mesh=mesh,
        in_specs=placed,
        out_specs=(P(None, "gx", "gy", "gz"), P("gx", "gy", "gz")),
        check_vma=False,
    )
```

```python
import jax
import jax.numpy as jnp
from jax import lax
from jax.experimental import pallas as pl
from jax.experimental.pallas import tpu as pltpu
from jax.sharding import PartitionSpec as P

sigma_table = (0.0, 3.0, 1.5, 6.0)
conduct_table = (1.0, 0.15, 0.05, 0.9)
capacity_table = (7.0, 2.0, 1.0, 6.0)
upwind_rate = 0.3
real_table = tuple(6.0 / (36.0 + s * s) for s in sigma_table)
imag_table = tuple(s / (36.0 + s * s) for s in sigma_table)
inverse_capacity = tuple(1.0 / c for c in capacity_table)

MESH = pl.DeviceIdType.MESH
LANES = 128
AXES = ("gx", "gy", "gz")
f32 = jnp.float32
bf16 = jnp.bfloat16


def lookup(material, table):
    first = jnp.where(material == 0, f32(table[0]), f32(table[1]))
    second = jnp.where(material == 2, f32(table[2]), f32(table[3]))
    return jnp.where(material < 2, first, second)


def halves(value):
    high = value.astype(bf16)
    return high, (value - high.astype(f32)).astype(bf16)


class Exchange:
    def __init__(self, number, sends, receives, faces):
        self.number, self.sends, self.receives, self.faces = number, sends, receives, faces

    def each(self):
        for at, (axis, (low_face, high_face), (low_halo, high_halo)) in enumerate(self.faces):
            me, count = lax.axis_index(axis), lax.axis_size(axis)
            up = pltpu.make_async_remote_copy(
                src_ref=high_face, dst_ref=low_halo,
                send_sem=self.sends.at[self.number, 2 * at],
                recv_sem=self.receives.at[self.number, 2 * at],
                device_id={axis: wrap(me + 1, count)}, device_id_type=MESH,
            )
            down = pltpu.make_async_remote_copy(
                src_ref=low_face, dst_ref=high_halo,
                send_sem=self.sends.at[self.number, 2 * at + 1],
                recv_sem=self.receives.at[self.number, 2 * at + 1],
                device_id={axis: wrap(me + count - 1, count)}, device_id_type=MESH,
            )
            yield me > 0, me < count - 1, up, down, low_halo, high_halo

    def start(self, only=AXES):
        for (axis, _, _), (below, above, up, down, _, _) in zip(self.faces, self.each()):
            if axis in only:
                pl.when(above)(up.start)
                pl.when(below)(down.start)

    def wait(self):
        for below, above, up, down, low_halo, high_halo in self.each():
            pl.when(below)(up.wait_recv)
            pl.when(above)(down.wait_recv)

    def clear(self):
        for axis, _, (low_halo, high_halo) in self.faces:
            me, count = lax.axis_index(axis), lax.axis_size(axis)

            @pl.when(me == 0)
            def _():
                low_halo[...] = jnp.zeros(low_halo.shape, f32)

            @pl.when(me == count - 1)
            def _():
                high_halo[...] = jnp.zeros(high_halo.shape, f32)

    def drain(self):
        for below, above, up, down, _, _ in self.each():
            pl.when(above)(up.wait_send)
            pl.when(below)(down.wait_send)


def iota(shape, dim):
    return lax.broadcasted_iota(jnp.int32, shape, dim)


def wrap(value, count):
    return value & (count - 1) if count & (count - 1) == 0 else lax.rem(value, count)


def face_columns(planes):
    stacked = jnp.concatenate(planes, axis=0)
    depth = stacked.shape[1]
    low = jnp.transpose(stacked[:, :LANES])
    high = low if depth == LANES else jnp.transpose(stacked[:, depth - LANES:])
    return low[0:1, :], high[LANES - 1:LANES, :]


def halo_columns(low, high):
    sub = iota((LANES, LANES), 0)
    return jnp.transpose(jnp.where(sub == 0, low, jnp.where(sub == LANES - 1, high, f32(0.0))))


def column_shifts(plane, halo):
    rows, depth = plane.shape
    lane = iota((rows, depth), 1)
    if depth > LANES and halo.ndim:
        halo = jnp.concatenate([halo] * (depth // LANES), axis=1)
    return (
        jnp.where(lane == 0, halo, pltpu.roll(plane, 1, 1)),
        jnp.where(lane == depth - 1, halo, pltpu.roll(plane, depth - 1, 1)),
    )


def row_shifts(plane, low, high):
    rows, depth = plane.shape
    row = iota((rows, depth), 0)
    return (
        jnp.where(row == 0, low, pltpu.roll(plane, 1, 0)),
        jnp.where(row == rows - 1, high, pltpu.roll(plane, rows - 1, 0)),
    )


def kernel(
    vec_hbm, source_hbm, mag_hbm, idx_hbm, count_hbm, cell_hbm, temp_hbm, heat_hbm,
    potential_hbm, out_hbm,
    field0, field1, source, mag, idx, count_ref, cell, temp0, temp1, temp2, heat_mat, kcell, coef, rate,
    near, xh_m, ys_m, yh_m, zs_m, zh_m, xs_t, xh_t, partial, ys_t, yh_t, zs_t, zh_t,
    table, chosen, sent, landed, one_hot, v_high, v_low, heat,
    load_sems, halo_send, halo_recv, slot_send, slot_recv,
):
    _, size_x, size_y, size_z = source.shape
    heat_x, heat_y, heat_z = heat_mat.shape
    n_gx, n_gy = lax.axis_size("gx"), lax.axis_size("gy")
    ix, iy, iz, n_gz = lax.axis_index("gx"), lax.axis_index("gy"), lax.axis_index("gz"), lax.axis_size("gz")
    group, here = n_gx * n_gy, ix * n_gy + iy

    loads = [
        pltpu.make_async_copy(src, dst, load_sems.at[at])
        for at, (src, dst) in enumerate(
            [
                (vec_hbm, field0.at[:, pl.ds(1, size_x)]),
                (temp_hbm, temp0.at[pl.ds(1, heat_x)]),
                (heat_hbm, heat_mat),
                (mag_hbm, mag),
                (source_hbm, source),
                (idx_hbm.at[0], idx),
                (cell_hbm.at[0], cell),
                (count_hbm, count_ref),
            ]
        )
    ]
    for load in loads:
        load.start()

    barrier = pltpu.get_barrier_semaphore()

    def greet(device):
        pl.semaphore_signal(barrier, inc=1, device_id=device, device_id_type=MESH)

    for step in range(1, n_gy):
        greet({"gy": wrap(iy + step, n_gy)})

    @pl.loop(1, n_gx)
    def _(step):
        for other in range(n_gy):
            greet({"gx": wrap(ix + step, n_gx), "gy": other})

    @pl.when(iz > 0)
    def _():
        greet({"gz": wrap(iz + n_gz - 1, n_gz)})

    @pl.when(iz < n_gz - 1)
    def _():
        greet({"gz": wrap(iz + 1, n_gz)})

    def faces(x_low, x_high, x_low_halo, x_high_halo, ys, yh, zs, zh, at):
        return [
            ("gx", (x_low, x_high), (x_low_halo, x_high_halo)),
            ("gy", (ys.at[at, 0], ys.at[at, 1]), (yh.at[at, 0], yh.at[at, 1])),
            ("gz", (zs.at[at, 0], zs.at[at, 1]), (zh.at[at, 0], zh.at[at, 1])),
        ]

    def mag_round(number, field):
        return Exchange(
            number, halo_send, halo_recv,
            faces(
                field.at[:, 1], field.at[:, size_x], xh_m.at[number, 0], xh_m.at[number, 1],
                ys_m, yh_m, zs_m, zh_m, number,
            ),
        )

    def heat_round(number, at, state):
        return Exchange(
            number, halo_send, halo_recv,
            faces(
                state.at[1], state.at[heat_x], xh_t.at[at, 0], xh_t.at[at, 1],
                ys_t, yh_t, zs_t, zh_t, at,
            ),
        )

    round0 = mag_round(0, field0)
    round1 = mag_round(1, field1)
    both = pl.ds(0, 2)
    round_t = Exchange(
        2, halo_send, halo_recv,
        faces(
            xs_t.at[0], xs_t.at[1], xh_t.at[both, 0], xh_t.at[both, 1],
            ys_t, yh_t, zs_t, zh_t, both,
        ),
    )
    round_1 = heat_round(4, 2, temp1)
    round_2 = heat_round(5, 3, temp2)
    rounds = (round0, round1, round_t, round_1, round_2)
    for each in rounds:
        each.clear()
    for field in (field0, field1):
        for x in (0, size_x + 1):
            field[:, x] = jnp.zeros((2, size_y, size_z), f32)
    for state in (temp1, temp2):
        for x in (0, heat_x + 1):
            state[x] = jnp.zeros((heat_y, heat_z), f32)

    block = LANES // size_y
    block_t = LANES // heat_y

    def pack_mag(at, j, part, planes):
        for i, plane in enumerate(planes):
            ys_m[at, 0, part, j * block + i] = plane[0:1, :]
            ys_m[at, 1, part, j * block + i] = plane[size_y - 1:size_y, :]
        zs_m[at, 0, part, j], zs_m[at, 1, part, j] = face_columns(planes)

    def pack_heat(at, j, planes):
        for i, plane in enumerate(planes):
            ys_t[at, 0, j * block_t + i] = plane[0:1, :]
            ys_t[at, 1, j * block_t + i] = plane[heat_y - 1:heat_y, :]

    def send_heat(each, packed):
        each.start(("gx", "gy"))

        @pl.loop(0, heat_x // block_t)
        def _(j):
            for at, state in packed:
                planes = [state[j * block_t + i + 1] for i in range(block_t)]
                zs_t[at, 0, j], zs_t[at, 1, j] = face_columns(planes)

        each.start(("gz",))

    loads[0].wait()

    @pl.loop(0, size_x // block)
    def _(j):
        for part in range(2):
            pack_mag(0, j, part, [field0[part, j * block + i + 1] for i in range(block)])

    pl.semaphore_wait(barrier, group - 1 + (iz > 0).astype(jnp.int32) + (iz < n_gz - 1).astype(jnp.int32))
    round0.start()

    loads[1].wait()
    loads[2].wait()

    @pl.loop(0, heat_x // block_t)
    def _(j):
        planes = []
        for i in range(block_t):
            x = j * block_t + i
            planes.append(lookup(heat_mat[x], conduct_table))
            kcell[x + 1] = planes[-1]
        pack_heat(1, j, planes)
        pack_heat(0, j, [temp0[j * block_t + i + 1] for i in range(block_t)])

    for at, state in enumerate((temp0, kcell)):
        xs_t[0, at] = state[1]
        xs_t[1, at] = state[heat_x]
    send_heat(round_t, ((0, temp0), (1, kcell)))

    def add_near(field):
        @pl.loop(0, size_x // block)
        def _(j):
            for part in range(2):
                for i in range(block):
                    x = j * block + i
                    plane = field[part, x + 1]
                    low_y, high_y = row_shifts(plane, f32(0.0), f32(0.0))
                    low_z, high_z = column_shifts(plane, f32(0.0))
                    near[part, x] = (field[part, x] + field[part, x + 2]) + (low_y + high_y) + (low_z + high_z)

    add_near(field0)
    for load in loads[3:]:
        load.wait()

    row_m = iota((size_y, size_z), 0)

    def add_planes(at):
        for part in range(2):
            near[part, 0] += xh_m[at, 0, part]
            near[part, size_x - 1] += xh_m[at, 1, part]

    def relaxed(at, j):
        columns = [halo_columns(zh_m[at, 0, part, j], zh_m[at, 1, part, j]) for part in range(2)]
        result = ([], [])
        for i in range(block):
            x = j * block + i
            total = []
            for part in range(2):
                rows = jnp.where(
                    row_m == 0, yh_m[at, 0, part, x], jnp.where(row_m == size_y - 1, yh_m[at, 1, part, x], f32(0.0))
                )
                total.append(
                    (source[part, x] + near[part, x]) + (rows + columns[part][i * size_y:(i + 1) * size_y, :])
                )
            material = mag[x]
            real, imag = lookup(material, real_table), lookup(material, imag_table)
            result[0].append(real * total[0] + imag * total[1])
            result[1].append(real * total[1] - imag * total[0])
        return result

    round0.wait()
    add_planes(0)

    @pl.loop(0, size_x // block)
    def _(j):
        for part, planes in enumerate(relaxed(0, j)):
            for i, plane in enumerate(planes):
                field1[part, j * block + i + 1] = plane
            pack_mag(1, j, part, planes)

    round1.start()

    round_t.wait()
    for at, state in enumerate((temp0, kcell)):
        state[0] = xh_t[at, 0]
        state[heat_x + 1] = xh_t[at, 1]

    def neighbours(at, state, j):
        columns = halo_columns(zh_t[at, 0, j], zh_t[at, 1, j])
        for i in range(block_t):
            x = j * block_t + i
            plane = state[x + 1]
            low_y, high_y = row_shifts(plane, yh_t[at, 0, x], yh_t[at, 1, x])
            low_z, high_z = column_shifts(plane, columns[i * heat_y:(i + 1) * heat_y, :])
            yield x, plane, (state[x], state[x + 2], low_y, high_y, low_z, high_z)

    @pl.loop(0, heat_x // block_t)
    def _(j):
        for (x, conduct, beside), (_, plane, around) in zip(neighbours(1, kcell, j), neighbours(0, temp0, j)):
            material = heat_mat[x]
            inverse = lookup(material, inverse_capacity)
            upwind = jnp.where(material == 1, f32(upwind_rate), f32(0.0))
            twice = (2.0 * inverse) * conduct
            centre = 1.0 - upwind
            total = jnp.zeros(plane.shape, f32)
            for side in range(6):
                weight = twice * beside[side] / (conduct + beside[side])
                centre = centre - weight
                if side == 4:
                    weight = weight + upwind
                coef[side, x] = weight
                total = total + weight * around[side]
            coef[6, x] = centre
            rate[x] = inverse
            temp1[x + 1] = total + centre * plane

    add_near(field1)
    round1.wait()
    add_planes(1)
    round0.drain()

    @pl.loop(0, size_x // block)
    def _(j):
        losses = []
        for i, planes in enumerate(zip(*relaxed(1, j))):
            x = j * block + i
            field0[0, x + 1] = planes[0]
            field0[1, x + 1] = planes[1]
            losses.append(
                (0.5 * lookup(mag[x], sigma_table)) * (planes[0] * planes[0] + planes[1] * planes[1])
            )
        high, low = halves(jnp.transpose(jnp.concatenate(losses, axis=0)))
        at = pl.ds(pl.multiple_of(j * LANES, LANES), LANES)
        table[0:size_z, at] = high
        table[size_z:2 * size_z, at] = low

    store_potential = pltpu.make_async_copy(
        field0.at[:, pl.ds(1, size_x)], potential_hbm, load_sems.at[8]
    )
    store_potential.start()

    table_rows = size_x * size_y
    width = n_gy * LANES
    slot = iota((1, LANES), 1)
    row16 = lax.broadcasted_iota(jnp.int16, (table_rows, LANES), 0)
    sub_z = iota((size_z, LANES), 0)

    def slot_copy(gx, gy):
        return pltpu.make_async_remote_copy(
            src_ref=sent.at[gx * n_gy + gy], dst_ref=landed.at[here],
            send_sem=slot_send, recv_sem=slot_recv.at[ix],
            device_id={"gx": gx, "gy": gy}, device_id_type=MESH,
        )

    def slots_from(gx, count):
        rows = landed.at[pl.ds(gx * n_gy, count)]
        return pltpu.make_async_remote_copy(
            src_ref=rows, dst_ref=rows, send_sem=slot_send, recv_sem=slot_recv.at[gx],
            device_id={"gx": wrap(ix + 1, n_gx)}, device_id_type=MESH,
        )

    @pl.loop(0, n_gx)
    def _(step):
        target = wrap(ix + step + 1, n_gx)
        first = target * n_gy
        cells = []
        for p in range(n_gy):
            wanted = jnp.where(slot < count_ref[0, first + p], idx[pl.ds(first + p, 1), :], -1)
            cells.append(wanted)
            row = jnp.broadcast_to(lax.shift_right_arithmetic(wanted, 7).astype(jnp.int16), (table_rows, LANES))
            chosen[:, LANES * p:LANES * (p + 1)] = jnp.where(row16 == row, jnp.ones((), bf16), jnp.zeros((), bf16))
        found = jnp.dot(table[...], chosen[...], preferred_element_type=f32)
        found = found[:size_z] + found[size_z:]
        for p in range(n_gy):
            hit = sub_z == (cells[p] & (size_z - 1))
            sent[first + p] = jnp.sum(
                jnp.where(hit, found[:, LANES * p:LANES * (p + 1)], 0.0), axis=0, keepdims=True
            )
        for p in range(n_gy):
            @pl.when(first + p != here)
            def _():
                slot_copy(target, p).start()

    landed[here] = sent[here]

    row_h = lax.broadcasted_iota(jnp.int16, (heat_x * heat_y, LANES), 0)
    row_z = lax.broadcasted_iota(jnp.int16, (heat_z, LANES), 0)
    shift = heat_z.bit_length() - 1
    heat[...] = jnp.zeros(heat.shape, f32)
    per = one_hot.shape[1] // LANES // n_gy
    zero16 = jnp.zeros((), bf16)
    transposed = (((1,), (1,)), ((), ()))

    @pl.loop(0, n_gx // per)
    def _(step):
        peers = []
        for k in range(per):
            gx = wrap(ix + 2 * n_gx - 1 - (step * per + k), n_gx)

            @pl.when(gx != ix)
            def _():
                slots_from(gx, n_gy).wait_recv()

            @pl.when(gx == ix)
            def _():
                slots_from(gx, n_gy - 1).wait_recv()

            peers += [gx * n_gy + gy for gy in range(n_gy)]

        for p, peer in enumerate(peers):
            target = cell[pl.ds(peer, 1), :]
            high, low = halves(landed[peer])
            at = slice(LANES * p, LANES * (p + 1))
            row = jnp.broadcast_to(lax.shift_right_logical(target, shift).astype(jnp.int16), row_h.shape)
            one_hot[:, at] = jnp.where(row_h == row, jnp.ones((), bf16), zero16)
            hit = row_z == jnp.broadcast_to((target & (heat_z - 1)).astype(jnp.int16), row_z.shape)
            v_high[:, at] = jnp.where(hit, jnp.broadcast_to(high, row_z.shape), zero16)
            v_low[:, at] = jnp.where(hit, jnp.broadcast_to(low, row_z.shape), zero16)
        heat[...] += lax.dot_general(
            one_hot[...], v_high[...], transposed, preferred_element_type=f32
        ) + lax.dot_general(one_hot[...], v_low[...], transposed, preferred_element_type=f32)

    @pl.loop(0, heat_x // block_t)
    def _(j):
        planes = []
        for i in range(block_t):
            x = j * block_t + i
            gain = heat[pl.ds(pl.multiple_of(x * heat_y, heat_y), heat_y), :] * rate[x]
            rate[x] = gain
            planes.append(temp1[x + 1] + gain)
            temp1[x + 1] = planes[-1]
        pack_heat(2, j, planes)

    send_heat(round_1, ((2, temp1),))

    row_t = iota((heat_y, heat_z), 0)
    depth_t = iota((heat_y, heat_z), 1)

    def step_near(state):
        @pl.loop(0, heat_x // block_t)
        def _(j):
            for i in range(block_t):
                x = j * block_t + i
                plane = state[x + 1]
                around = (
                    (state[x], state[x + 2])
                    + row_shifts(plane, f32(0.0), f32(0.0))
                    + column_shifts(plane, f32(0.0))
                )
                total = coef[6, x] * plane + rate[x]
                for side, other in enumerate(around):
                    total = total + coef[side, x] * other
                partial[x] = total

    def add_ends(at):
        partial[0] += coef[0, 0] * xh_t[at, 0]
        partial[heat_x - 1] += coef[1, heat_x - 1] * xh_t[at, 1]

    def stepped(at, j):
        columns = halo_columns(zh_t[at, 0, j], zh_t[at, 1, j])
        columns = jnp.concatenate([columns] * (heat_z // LANES), axis=1)
        for i in range(block_t):
            x = j * block_t + i
            column = columns[i * heat_y:(i + 1) * heat_y, :]
            low_y, high_y = coef[2, x] * yh_t[at, 0, x], coef[3, x] * yh_t[at, 1, x]
            low_z, high_z = coef[4, x] * column, coef[5, x] * column
            zero = f32(0.0)
            rows = jnp.where(row_t == 0, low_y, jnp.where(row_t == heat_y - 1, high_y, zero))
            ends = jnp.where(depth_t == 0, low_z, jnp.where(depth_t == heat_z - 1, high_z, zero))
            yield x, partial[x] + (rows + ends)

    step_near(temp1)
    for each in (round1, round_t):
        each.drain()
    everyone = sent.at[pl.ds(0, group - 1)]
    pltpu.make_async_remote_copy(
        src_ref=everyone, dst_ref=everyone, send_sem=slot_send, recv_sem=slot_recv.at[0],
        device_id={"gx": wrap(ix + 1, n_gx)}, device_id_type=MESH,
    ).wait_send()
    store_potential.wait()
    round_1.wait()
    add_ends(2)

    @pl.loop(0, heat_x // block_t)
    def _(j):
        planes = []
        for x, plane in stepped(2, j):
            temp2[x + 1] = plane
            planes.append(plane)
        pack_heat(3, j, planes)

    send_heat(round_2, ((3, temp2),))
    step_near(temp2)
    round_1.drain()
    round_2.wait()
    add_ends(3)

    @pl.loop(0, heat_x // block_t)
    def _(j):
        for x, plane in stepped(3, j):
            temp0[x + 1] = plane

    store_temp = pltpu.make_async_copy(temp0.at[pl.ds(1, heat_x)], out_hbm, load_sems.at[9])
    store_temp.start()
    round_2.drain()

    store_temp.wait()


def finish(potential_in, temp_in, potential_out, temp_out, potential, temp, sems):
    pieces = 4
    size_x = potential.shape[1] // pieces
    steps = []
    for piece in range(pieces):
        at = pl.ds(piece * size_x, size_x)
        steps.append((potential_in.at[:, at], potential.at[:, at], potential_out.at[:, at]))
    steps.append((temp_in, temp, temp_out))
    arrive = [pltpu.make_async_copy(a, b, sems.at[0, k]) for k, (a, b, _) in enumerate(steps)]
    leave = [pltpu.make_async_copy(b, c, sems.at[1, k]) for k, (_, b, c) in enumerate(steps)]
    for copy in arrive:
        copy.start()
    for copy, out in zip(arrive, leave):
        copy.wait()
        out.start()
    for out in leave:
        out.wait()


def shards(vec_prev, source, mag_mat, send_idx, send_count, recv_cell, temp, heat_mat):
    _, size_x, size_y, size_z = vec_prev.shape
    heat_x, heat_y, heat_z = temp.shape
    n_gx, n_gy = lax.axis_size("gx"), lax.axis_size("gy")
    group = n_gx * n_gy
    per = min(2, n_gx) * n_gy
    vmem = pltpu.VMEM
    anywhere = pl.BlockSpec(memory_space=pl.ANY)
    results = pl.pallas_call(
        kernel,
        out_shape=(
            jax.ShapeDtypeStruct(vec_prev.shape, f32),
            jax.ShapeDtypeStruct(temp.shape, f32),
        ),
        in_specs=[anywhere] * 8,
        out_specs=(anywhere, anywhere),
        scratch_shapes=[
            vmem((2, size_x + 2, size_y, size_z), f32),
            vmem((2, size_x + 2, size_y, size_z), f32),
            vmem(source.shape, f32),
            vmem(mag_mat.shape, jnp.int32),
            vmem(send_idx.shape[1:], jnp.int32),
            pltpu.SMEM(send_count.shape, jnp.int32),
            vmem(recv_cell.shape[1:], jnp.int32),
            vmem((heat_x + 2, heat_y, heat_z), f32),
            vmem((heat_x + 2, heat_y, heat_z), f32),
            vmem((heat_x + 2, heat_y, heat_z), f32),
            vmem(heat_mat.shape, jnp.int32),
            vmem((heat_x + 2, heat_y, heat_z), f32),
            vmem((7, heat_x, heat_y, heat_z), f32),
            vmem((heat_x, heat_y, heat_z), f32),
            vmem(source.shape, f32),
            vmem((2, 2, 2, size_y, size_z), f32),
            vmem((2, 2, 2, size_x, 1, size_z), f32),
            vmem((2, 2, 2, size_x, 1, size_z), f32),
            vmem((2, 2, 2, size_x * size_y // LANES, 1, LANES), f32),
            vmem((2, 2, 2, size_x * size_y // LANES, 1, LANES), f32),
            vmem((2, 2, heat_y, heat_z), f32),
            vmem((4, 2, heat_y, heat_z), f32),
            vmem((heat_x, heat_y, heat_z), f32),
            vmem((4, 2, heat_x, 1, heat_z), f32),
            vmem((4, 2, heat_x, 1, heat_z), f32),
            vmem((4, 2, heat_x * heat_y // LANES, 1, LANES), f32),
            vmem((4, 2, heat_x * heat_y // LANES, 1, LANES), f32),
            vmem((2 * size_z, size_x * size_y), bf16),
            vmem((size_x * size_y, n_gy * LANES), bf16),
            vmem((group, 1, LANES), f32),
            vmem((group, 1, LANES), f32),
            vmem((heat_x * heat_y, per * LANES), bf16),
            vmem((heat_z, per * LANES), bf16),
            vmem((heat_z, per * LANES), bf16),
            vmem((heat_x * heat_y, heat_z), f32),
            pltpu.SemaphoreType.DMA((10,)),
            pltpu.SemaphoreType.DMA((6, 6)),
            pltpu.SemaphoreType.DMA((6, 6)),
            pltpu.SemaphoreType.DMA,
            pltpu.SemaphoreType.DMA((n_gx,)),
        ],
        compiler_params=pltpu.CompilerParams(
            collective_id=0, has_side_effects=True, vmem_limit_bytes=60 << 20
        ),
    )(vec_prev, source, mag_mat, send_idx, send_count, recv_cell, temp, heat_mat)
    return pl.pallas_call(
        finish,
        out_shape=tuple(jax.ShapeDtypeStruct(result.shape, f32) for result in results),
        in_specs=[anywhere] * 2,
        out_specs=(anywhere, anywhere),
        scratch_shapes=[
            vmem(vec_prev.shape, f32),
            vmem(temp.shape, f32),
            pltpu.SemaphoreType.DMA((2, 5)),
        ],
        compiler_params=pltpu.CompilerParams(vmem_limit_bytes=60 << 20),
    )(*results)


def solution(mesh):
    placed = (
        P(None, "gx", "gy", "gz"),
        P(None, "gx", "gy", "gz"),
        P("gx", "gy", "gz"),
        P(("gx", "gy", "gz"), None, None),
        P(("gx", "gy", "gz"), None),
        P(("gx", "gy", "gz"), None, None),
        P("gx", "gy", "gz"),
        P("gx", "gy", "gz"),
    )
    return jax.shard_map(
        shards,
        mesh=mesh,
        in_specs=placed,
        out_specs=(P(None, "gx", "gy", "gz"), P("gx", "gy", "gz")),
        check_vma=False,
    )
```
